256 devices in a mesh: row: 16 (over z, core), col: 16 (over x, y).
Axes of the slice: x: 4, y: 4, z: 8, core: 2. Of those that a mesh axis runs over, the one named last changes fastest.
Arguments:
- prior_factor: float32 [1024, 196608], P('row', 'col'), may hold values from -0.013671875 to 0.013671875
- prior_solution: float32 [64, 196608], P(None, 'col'), may hold values from -6 to 6
- panel_lower: float32 [1024, 1024], P('row'), may hold values from -1 to 1, as said below
- tile_inverse: float32 [1024, 64], P('row'), may hold values from -1 to 2, as said below
- panel_target: float32 [64, 1024], P(None, 'row'), may hold values from -6 to 6
- next_prior: float32 [1024, 196608], P('row', 'col'), may hold values from -0.013671875 to 0.013671875
- next_under: float32 [1024, 1024], P('row', 'col'), may hold values from -0.1875 to 0.1875
- next_target: float32 [64, 1024], P(None, 'row'), may hold values from -6 to 6
Outputs:
- panel_solution: float32 [64, 1024], P(None, 'row')
- next_remainder: float32 [64, 1024], P(None, 'row')
The draws below stay inside these ranges and needn't reach their ends.
Inputs may be any that keep to these rules, and one draw needn't show every extreme that they name: `panel_lower`: zero in every column of the tile that holds the row and in all later columns; the other entries are independent. `tile_inverse`: each tile is lower triangular with diagonal entries between 0.6 and 1.6.
All inputs are finite; a program needn't handle non-finite values.
Results may differ from the reference program's by a relative error of at most 0.00011.
Values sent between devices are 32-bit elements; how exact they have to be, the bound alone decides.
A program may use at most 64 MiB of HBM per device.

```python
import jax
import jax.numpy as jnp
from jax import lax

NB = 1024
TB = 64
NRHS = 64
KPREV = 196608


def draw_panel_lower(key, part):
    key = jax.random.fold_in(key, 11)
    values = jax.random.uniform(key, (NB, NB), jnp.float32, -1.0, 1.0) * (0.9 / NB ** 0.5)
    rows = jnp.arange(NB)[:, None] // TB
    columns = jnp.arange(NB)[None, :] // TB
    return jnp.where(columns < rows, values, 0.0).astype(jnp.float32)


def draw_tile_inverse(key, part):
    key = jax.random.fold_in(key, 23)
    first_key, second_key = jax.random.split(key)
    lower = jax.random.uniform(first_key, (NB, TB), jnp.float32, -1.0, 1.0) * (0.9 / TB ** 0.5)
    diagonal = jax.random.uniform(second_key, (NB, TB), jnp.float32, 0.6, 1.6)
    local_row = jnp.arange(NB)[:, None] % TB
    column = jnp.arange(TB)[None, :]
    result = jnp.where(column < local_row, lower, 0.0)
    result = jnp.where(column == local_row, diagonal, result)
    return result.astype(jnp.float32)


def steps_of(own_key, extent, shards, low, largest):
    level, own = 1.0, jax.random.fold_in(own_key, 6)
    for axis_at, blocks in shards:
        steps = jnp.exp(jax.random.uniform(jax.random.fold_in(own, axis_at), (blocks,), jnp.float32, low / len(shards), largest / len(shards)))
        level = level * jnp.repeat(steps, extent[axis_at] // blocks).reshape([-1 if axis == axis_at else 1 for axis in range(len(extent))])
    return level


def scatter_about(rng, dims, width, reach, cuts=(), kind=jnp.bfloat16):
    factor_of = steps_of(rng, dims, cuts, -0.22, 0.18) if cuts else 1.0
    drawn = jax.random.normal(rng, dims, jnp.float32) * width * factor_of
    return jnp.minimum(jnp.maximum(drawn, -reach), reach).astype(kind)


def setup_inputs(seed: int = 0) -> dict:
    seeds = jax.random.split(jax.random.key(seed), 9)
    return {
        "prior_factor": scatter_about(seeds[0], (NB, KPREV), KPREV ** -0.5, 0.013671875, ((0, 16), (1, 16)), jnp.float32),
        "prior_solution": scatter_about(seeds[1], (NRHS, KPREV), 1.0, 6.0, ((1, 16),), jnp.float32),
        "panel_lower": draw_panel_lower(jax.random.fold_in(seeds[8], 71), 0),
        "tile_inverse": draw_tile_inverse(jax.random.fold_in(seeds[8], 71), 0),
        "panel_target": scatter_about(seeds[4], (NRHS, NB), 1.0, 6.0, ((1, 16),), jnp.float32),
        "next_prior": scatter_about(seeds[5], (NB, KPREV), KPREV ** -0.5, 0.013671875, ((0, 16), (1, 16)), jnp.float32),
        "next_under": scatter_about(seeds[6], (NB, NB), NB ** -0.5, 0.1875, ((0, 16), (1, 16)), jnp.float32),
        "next_target": scatter_about(seeds[7], (NRHS, NB), 1.0, 6.0, ((1, 16),), jnp.float32),
    }


def contract(left, right):
    return lax.dot_general(left, right, (((1,), (1,)), ((), ())), precision=lax.Precision.HIGHEST, preferred_element_type=jnp.float32)


def reference(prior_factor, prior_solution, panel_lower, tile_inverse, panel_target, next_prior, next_under, next_target):
    earlier = contract(prior_solution, prior_factor)
    remaining = panel_target - earlier
    solved = jnp.zeros((NRHS, NB), jnp.float32)
    for tile in range(NB // TB):
        first = tile * TB
        current = remaining[:, first:first + TB] - contract(solved, panel_lower[first:first + TB, :])
        block = contract(current, tile_inverse[first:first + TB, :])
        solved = solved.at[:, first:first + TB].set(block)
    remainder = next_target - contract(prior_solution, next_prior) - contract(solved, next_under)
    return solved, remainder
```

```python
import jax
import jax.numpy as jnp
from jax import lax
from jax.experimental import pallas as pl
from jax.experimental.pallas import tpu as pltpu
from jax.sharding import PartitionSpec as P

MESH = pl.DeviceIdType.MESH
TILE = 64
CHUNK = 1024
F32 = jnp.float32
BF16 = jnp.bfloat16


def nt(a, b):
    return lax.dot_general(a, b, (((1,), (1,)), ((), ())), preferred_element_type=F32)


def nn(a, b):
    return lax.dot_general(a, b, (((1,), (0,)), ((), ())), preferred_element_type=F32)


def parts(a):
    high = a.astype(BF16)
    return high, (a - high.astype(F32)).astype(BF16)


def product(a, b, dot):
    a_high, a_low = parts(a)
    b_high, b_low = parts(b)
    return dot(a_high, b_high) + (dot(a_high, b_low) + dot(a_low, b_high))


def pack(a):
    return jnp.concatenate([a[:32], a[32:]], axis=1)


def unpack(a):
    return jnp.concatenate([a[:, :64], a[:, 64:]], axis=0)


def unpack_pair(a, b):
    return jnp.concatenate(
        [
            jnp.concatenate([a[:, :64], b[:, :64]], axis=1),
            jnp.concatenate([a[:, 64:], b[:, 64:]], axis=1),
        ],
        axis=0,
    )


def kernel(
    factor_hbm,
    prior_hbm,
    lower_hbm,
    inverse_hbm,
    target_hbm,
    next_hbm,
    under_hbm,
    next_target_hbm,
    solution_ref,
    remainder_ref,
    factor,
    prior,
    nexts,
    lower,
    inverse,
    target,
    under,
    next_target,
    whole,
    panel_parts,
    next_parts,
    under_parts,
    reduced,
    load_sem,
    small_sem,
    col_send,
    col_recv,
    z_send,
    z_recv,
    pair_send,
    pair_recv,
    a_send,
    a_recv,
    b_send,
    b_recv,
    c_send,
    c_recv,
):
    r = lax.axis_index("row")
    c = lax.axis_index("col")
    z, core = r // 2, r % 2
    x, y = c // 4, c % 4
    quarter = (x + 2 * y) % 4
    sibling = (2 * z + 1 - core, c)
    chunks = factor.shape[1] // CHUNK

    small = []
    for i, (source, destination) in enumerate(
        (
            (lower_hbm, lower),
            (inverse_hbm, inverse),
            (under_hbm, under),
            (target_hbm, target),
            (next_target_hbm, next_target),
        )
    ):
        copy = pltpu.make_async_copy(source, destination, small_sem.at[i])
        copy.start()
        small.append(copy)

    def loads(i):
        at = pl.ds(pl.multiple_of(i * CHUNK, CHUNK), CHUNK)
        return [
            pltpu.make_async_copy(source.at[:, at], destination.at[:, at], load_sem.at[j, i])
            for j, (source, destination) in enumerate(
                ((prior_hbm, prior), (factor_hbm, factor), (next_hbm, nexts))
            )
        ]

    @pl.loop(0, chunks)
    def _(i):
        for copy in loads(i):
            copy.start()

    barrier = pltpu.get_barrier_semaphore()

    @pl.loop(1, 16)
    def _(k):
        pl.semaphore_signal(barrier, inc=1, device_id=(r, (c + k) % 16), device_id_type=MESH)

    @pl.loop(1, 8)
    def _(k):
        pl.semaphore_signal(
            barrier, inc=1, device_id=(2 * ((z + k) % 8) + core, c), device_id_type=MESH
        )

    pl.semaphore_signal(barrier, inc=1, device_id=sibling, device_id_type=MESH)

    for copy in small:
        copy.wait()
    own_rows = pl.ds(pl.multiple_of(r * TILE, TILE), TILE)
    whole[own_rows, :] = product(inverse[...], lower[...], nn)
    under_parts[c] = pack(under[...])

    def add(i, total):
        for copy in loads(i):
            copy.wait()
        at = pl.ds(pl.multiple_of(i * CHUNK, CHUNK), CHUNK)
        s_high, s_low = parts(prior[:, at])
        f_high, f_low = parts(factor[:, at])
        n_high, n_low = parts(nexts[:, at])
        return total + nt(
            jnp.concatenate([s_high, s_low], axis=0),
            jnp.concatenate([f_high, n_high, f_low, n_low], axis=0),
        )

    total = lax.fori_loop(0, chunks, add, jnp.zeros((128, 256), F32))
    sums = (total[:64, :128] + total[64:, 128:]) + (total[:64, 128:] + total[64:, :128])
    panel_parts[c] = pack(sums[:, :64])
    next_parts[c] = pack(sums[:, 64:])

    pl.semaphore_wait(barrier, 23)

    def over_col(buffer, i, k):
        return pltpu.make_async_remote_copy(
            src_ref=buffer.at[c],
            dst_ref=buffer.at[c],
            send_sem=col_send.at[i, k],
            recv_sem=col_recv.at[i, c],
            device_id=(r, (c + k) % 16),
            device_id_type=MESH,
        )

    def from_col(buffer, i, k):
        source = (c + k) % 16
        return pltpu.make_async_remote_copy(
            src_ref=buffer.at[source],
            dst_ref=buffer.at[source],
            send_sem=col_send.at[i, k],
            recv_sem=col_recv.at[i, source],
            device_id=(r, source),
            device_id_type=MESH,
        )

    @pl.loop(1, 16)
    def _(k):
        over_col(panel_parts, 0, k).start()

    def rows_of(tile, q, n, count=16):
        return whole.at[pl.ds(pl.multiple_of(tile * TILE + q * 16, 16), count), pl.ds(0, 128 * n)]

    def by_width(width, body):
        for n in range(1, 9):
            pl.when(width == n)(lambda n=n: body(n))

    def a_copy(n, k):
        return pltpu.make_async_remote_copy(
            src_ref=rows_of(r, quarter, n),
            dst_ref=rows_of(r, quarter, n),
            send_sem=a_send.at[k],
            recv_sem=a_recv.at[z],
            device_id=(2 * ((z + k) % 8) + core, c),
            device_id_type=MESH,
        )

    def c_copy(n, at, q, count):
        tile = 2 * at + core
        return pltpu.make_async_remote_copy(
            src_ref=rows_of(tile, q, n, count),
            dst_ref=rows_of(tile, q, n, count),
            send_sem=c_send.at[at, q],
            recv_sem=c_recv.at[at],
            device_id=sibling,
            device_id_type=MESH,
        )

    def distance(i):
        return (1 - i % 2) * (1 + i // 2) + (i % 2) * (7 - i // 2)

    def send_own(n):
        @pl.loop(0, 7)
        def _(i):
            a_copy(n, distance(i)).start()

        c_copy(n, z, 0, 64).start()

    by_width(z + core, send_own)

    @pl.loop(1, 16)
    def _(k):
        over_col(under_parts, 1, k).start()

    def b_copy(n, at, d, q):
        tile = 2 * at + core
        if d < 2:
            to = ((x + (1 if d == 0 else 3)) % 4) * 4 + y
        else:
            to = x * 4 + (y + 1 + 2 * (at % 2)) % 4
        return pltpu.make_async_remote_copy(
            src_ref=rows_of(tile, q, n),
            dst_ref=rows_of(tile, q, n),
            send_sem=b_send.at[d, at],
            recv_sem=b_recv.at[d, at],
            device_id=(r, to),
            device_id_type=MESH,
        )

    def a_wait(n, at):
        tile = 2 * at + core
        pltpu.make_async_remote_copy(
            src_ref=rows_of(tile, quarter, n),
            dst_ref=rows_of(tile, quarter, n),
            send_sem=a_send.at[0],
            recv_sem=a_recv.at[at],
            device_id=(tile, c),
            device_id_type=MESH,
        ).wait_recv()

    def forward(i, carry):
        at = (z + distance(i)) % 8

        def one(n):
            a_wait(n, at)
            for d in range(3):
                b_copy(n, at, d, quarter).start()
            c_copy(n, at, quarter, 16).start()

        by_width(at + core, one)
        return carry

    lax.fori_loop(0, 4, forward, 0)

    @pl.loop(1, 16)
    def _(k):
        from_col(panel_parts, 0, k).wait_recv()

    sum_1 = panel_parts[0]
    for k in range(1, 16):
        sum_1 = sum_1 + panel_parts[k]
    remaining = target[...] - unpack(sum_1)
    reduced[r] = pack(product(remaining, inverse[...], nt))

    def z_copy(k):
        return pltpu.make_async_remote_copy(
            src_ref=reduced.at[r],
            dst_ref=reduced.at[r],
            send_sem=z_send.at[k],
            recv_sem=z_recv.at[z],
            device_id=(2 * ((z + k) % 8) + core, c),
            device_id_type=MESH,
        )

    def pair_copy(at):
        return pltpu.make_async_remote_copy(
            src_ref=reduced.at[2 * at + core],
            dst_ref=reduced.at[2 * at + core],
            send_sem=pair_send.at[at],
            recv_sem=pair_recv.at[at],
            device_id=sibling,
            device_id_type=MESH,
        )

    @pl.loop(1, 8)
    def _(k):
        z_copy(k).start()

    pair_copy(z).start()

    lax.fori_loop(4, 7, forward, 0)

    @pl.loop(1, 16)
    def _(k):
        over_col(next_parts, 2, k).start()

    def others(i, carry):
        at = (z + distance(i)) % 8

        def one(n):
            for d, step in ((0, 3), (1, 1), (2, 2)):
                q = (quarter + step) % 4
                b_copy(n, at, d, q).wait_recv()
                c_copy(n, at, q, 16).start()

        by_width(at + core, one)
        return carry

    lax.fori_loop(0, 7, others, 0)

    @pl.loop(0, 7)
    def _(i):
        at = (z + distance(i)) % 8
        pltpu.make_async_remote_copy(
            src_ref=reduced.at[2 * at + core],
            dst_ref=reduced.at[2 * at + core],
            send_sem=z_send.at[0],
            recv_sem=z_recv.at[at],
            device_id=(2 * at + core, c),
            device_id_type=MESH,
        ).wait_recv()
        pair_copy(at).start()

    @pl.loop(1, 16)
    def _(k):
        from_col(under_parts, 1, k).wait_recv()

    @pl.loop(1, 16)
    def _(k):
        from_col(next_parts, 2, k).wait_recv()

    @pl.loop(0, 8)
    def _(at):
        tile = 2 * at + 1 - core

        def one(n):
            pltpu.make_async_remote_copy(
                src_ref=rows_of(tile, 0, n, 64),
                dst_ref=rows_of(tile, 0, n, 64),
                send_sem=c_send.at[at, 0],
                recv_sem=c_recv.at[at],
                device_id=sibling,
                device_id_type=MESH,
            ).wait_recv()

        by_width(at + 1 - core, one)
        pltpu.make_async_remote_copy(
            src_ref=reduced.at[tile],
            dst_ref=reduced.at[tile],
            send_sem=pair_send.at[at],
            recv_sem=pair_recv.at[at],
            device_id=sibling,
            device_id_type=MESH,
        ).wait_recv()

    @pl.loop(1, 16)
    def _(k):
        over_col(panel_parts, 0, k).wait_send()
        over_col(under_parts, 1, k).wait_send()
        over_col(next_parts, 2, k).wait_send()

    @pl.loop(1, 8)
    def _(k):
        z_copy(k).wait_send()

    @pl.loop(0, 8)
    def _(at):
        pair_copy(at).wait_send()

    def own_sent(n):
        @pl.loop(1, 8)
        def _(k):
            a_copy(n, k).wait_send()

        c_copy(n, z, 0, 64).wait_send()

    by_width(z + core, own_sent)

    @pl.loop(0, 7)
    def _(i):
        at = (z + distance(i)) % 8

        def one(n):
            for d in range(3):
                b_copy(n, at, d, quarter).wait_send()
            for q in range(4):
                c_copy(n, at, q, 16).wait_send()

        by_width(at + core, one)

    held = []
    for p in range(8):
        right = unpack_pair(reduced[2 * p], reduced[2 * p + 1])
        link = whole[128 * p + 64 : 128 * p + 128, 128 * p : 128 * p + 128]
        link = link[:, :64]
        held.append(
            jnp.concatenate(
                [right[:, :64], right[:, 64:] - product(right[:, :64], link, nt)], axis=1
            )
        )
        if p > 0:
            even = whole[128 * p : 128 * p + 64, : 128 * p]
            odd = whole[128 * p + 64 : 128 * p + 128, : 128 * p]
            whole[128 * p + 64 : 128 * p + 128, : 128 * p] = odd - product(link, even, nn)

    later = jnp.zeros((64, 64), F32)
    for p in range(8):
        solved = held[p]
        reduced[2 * p] = solved[:32]
        reduced[2 * p + 1] = solved[32:]
        if p < 7:
            change = product(
                solved, whole[128 * (p + 1) :, 128 * p : 128 * (p + 1)], nt
            )
            for m in range(p + 1, 8):
                at = 128 * (m - p - 1)
                held[m] = held[m] - change[:, at : at + 128]
        later = later + product(
            solved, unpack_pair(under_parts[2 * p], under_parts[2 * p + 1]), nt
        )

    mine = jnp.concatenate([reduced[2 * z], reduced[2 * z + 1]], axis=0)
    solution_ref[...] = jnp.where(core == 0, mine[:, :64], mine[:, 64:])
    sum_2 = next_parts[0]
    for k in range(1, 16):
        sum_2 = sum_2 + next_parts[k]
    remainder_ref[...] = next_target[...] - unpack(sum_2) - later


def local(*args):
    factor, prior, lower, inverse, target = args[:5]
    width = factor.shape[1]
    out = jax.ShapeDtypeStruct(target.shape, F32)
    return pl.pallas_call(
        kernel,
        out_shape=(out, out),
        in_specs=[pl.BlockSpec(memory_space=pltpu.HBM)] * 8,
        out_specs=(pl.BlockSpec(memory_space=pltpu.VMEM),) * 2,
        scratch_shapes=[
            pltpu.VMEM((64, width), F32),
            pltpu.VMEM((64, width), F32),
            pltpu.VMEM((64, width), F32),
            pltpu.VMEM((64, 1024), F32),
            pltpu.VMEM((64, 64), F32),
            pltpu.VMEM((64, 64), F32),
            pltpu.VMEM((64, 64), F32),
            pltpu.VMEM((64, 64), F32),
            pltpu.VMEM((1024, 1024), F32),
            pltpu.VMEM((16, 32, 128), F32),
            pltpu.VMEM((16, 32, 128), F32),
            pltpu.VMEM((16, 32, 128), F32),
            pltpu.VMEM((16, 32, 128), F32),
            pltpu.SemaphoreType.DMA((3, width // CHUNK)),
            pltpu.SemaphoreType.DMA((5,)),
            pltpu.SemaphoreType.DMA((3, 16)),
            pltpu.SemaphoreType.DMA((3, 16)),
            pltpu.SemaphoreType.DMA((8,)),
            pltpu.SemaphoreType.DMA((8,)),
            pltpu.SemaphoreType.DMA((8,)),
            pltpu.SemaphoreType.DMA((8,)),
            pltpu.SemaphoreType.DMA((8,)),
            pltpu.SemaphoreType.DMA((8,)),
            pltpu.SemaphoreType.DMA((3, 8)),
            pltpu.SemaphoreType.DMA((3, 8)),
            pltpu.SemaphoreType.DMA((8, 4)),
            pltpu.SemaphoreType.DMA((8,)),
        ],
        compiler_params=pltpu.CompilerParams(
            collective_id=0, has_side_effects=True, vmem_limit_bytes=60 * 1024 * 1024
        ),
    )(*args)


def solution(mesh):
    return jax.shard_map(
        local,
        mesh=mesh,
        in_specs=(
            P("row", "col"),
            P(None, "col"),
            P("row", None),
            P("row", None),
            P(None, "row"),
            P("row", "col"),
            P("row", "col"),
            P(None, "row"),
        ),
        out_specs=(P(None, "row"), P(None, "row")),
        check_vma=False,
    )
```

```python
import jax
import jax.numpy as jnp
from jax import lax
from jax.experimental import pallas as pl
from jax.experimental.pallas import tpu as pltpu
from jax.sharding import PartitionSpec as P

MESH = pl.DeviceIdType.MESH
TILE = 64
CHUNK = 2048
F32 = jnp.float32
BF16 = jnp.bfloat16


def nt(a, b):
    return lax.dot_general(a, b, (((1,), (1,)), ((), ())), preferred_element_type=F32)


def nn(a, b):
    return lax.dot_general(a, b, (((1,), (0,)), ((), ())), preferred_element_type=F32)


def parts(a):
    high = a.astype(BF16)
    return high, (a - high.astype(F32)).astype(BF16)


def product(a, b, dot):
    a_high, a_low = parts(a)
    b_high, b_low = parts(b)
    return dot(a_high, b_high) + (dot(a_high, b_low) + dot(a_low, b_high))


def pack(a):
    return jnp.concatenate([a[:32], a[32:]], axis=1)


def unpack(a):
    return jnp.concatenate([a[:, :64], a[:, 64:]], axis=0)


def unpack_pair(a, b):
    return jnp.concatenate(
        [
            jnp.concatenate([a[:, :64], b[:, :64]], axis=1),
            jnp.concatenate([a[:, 64:], b[:, 64:]], axis=1),
        ],
        axis=0,
    )


def kernel(
    factor_hbm,
    prior_hbm,
    lower_hbm,
    inverse_hbm,
    target_hbm,
    next_hbm,
    under_hbm,
    next_target_hbm,
    out_ref,
    prior,
    lower,
    small,
    whole,
    panel_parts,
    next_parts,
    under_parts,
    reduced,
    load_sem,
    small_sem,
    col_send,
    col_recv,
    z_sem,
    pair_sem,
    a_send,
    a_recv,
    b_send,
    b_recv,
    c_send,
    c_recv,
):
    r = lax.axis_index("row")
    c = lax.axis_index("col")
    z, core = r // 2, r % 2
    x, y = c // 4, c % 4
    quarter = (x + 2 * y) % 4
    sibling = (2 * z + 1 - core, c)
    chunks = prior.shape[1] // CHUNK

    pltpu.make_async_copy(lower_hbm, lower, small_sem.at[0]).start()
    for i, source in enumerate((inverse_hbm, under_hbm, target_hbm, next_target_hbm)):
        pltpu.make_async_copy(source, small.at[i], small_sem.at[1]).start()

    def columns(i):
        return pl.ds(pl.multiple_of(i * CHUNK, CHUNK), CHUNK)

    @pl.loop(0, chunks)
    def _(i):
        for j, source in enumerate((prior_hbm, factor_hbm, next_hbm)):
            pltpu.make_async_copy(
                source.at[:, columns(i)],
                prior.at[pl.ds(TILE * j, TILE), columns(i)],
                load_sem.at[i],
            ).start()

    barrier = pltpu.get_barrier_semaphore()

    @pl.loop(1, 16)
    def _(k):
        pl.semaphore_signal(barrier, inc=1, device_id=(r, (c + k) % 16), device_id_type=MESH)

    @pl.loop(1, 8)
    def _(k):
        pl.semaphore_signal(
            barrier, inc=1, device_id=(2 * ((z + k) % 8) + core, c), device_id_type=MESH
        )

    pl.semaphore_signal(barrier, inc=1, device_id=sibling, device_id_type=MESH)

    pltpu.make_async_copy(lower, lower, small_sem.at[0]).wait()
    pltpu.make_async_copy(small, small, small_sem.at[1]).wait()
    inverse, target, next_target = small.at[0], small.at[2], small.at[3]
    own_rows = pl.ds(pl.multiple_of(r * TILE, TILE), TILE)
    whole[own_rows, :] = product(inverse[...], lower[...], nn)
    under_parts[c] = pack(small[1])

    pl.semaphore_wait(barrier, 23)

    def over_col(buffer, i, k):
        return pltpu.make_async_remote_copy(
            src_ref=buffer.at[c],
            dst_ref=buffer.at[c],
            send_sem=col_send.at[i],
            recv_sem=col_recv.at[i],
            device_id=(r, (c + k) % 16),
            device_id_type=MESH,
        )

    def all_col(buffer, i):
        return pltpu.make_async_remote_copy(
            src_ref=buffer.at[pl.ds(0, 15)],
            dst_ref=buffer.at[pl.ds(0, 15)],
            send_sem=col_send.at[i],
            recv_sem=col_recv.at[i],
            device_id=(r, (c + 1) % 16),
            device_id_type=MESH,
        )

    def rows_of(tile, q, n, count=16):
        return whole.at[pl.ds(pl.multiple_of(tile * TILE + q * 16, 16), count), pl.ds(0, 128 * n)]

    def by_width(width, body):
        for n in range(1, 9):
            pl.when(width == n)(lambda n=n: body(n))

    def a_copy(n, k):
        return pltpu.make_async_remote_copy(
            src_ref=rows_of(r, quarter, n),
            dst_ref=rows_of(r, quarter, n),
            send_sem=a_send.at[0],
            recv_sem=a_recv.at[z],
            device_id=(2 * ((z + k) % 8) + core, c),
            device_id_type=MESH,
        )

    def c_copy(n, at, q, count):
        tile = 2 * at + core
        return pltpu.make_async_remote_copy(
            src_ref=rows_of(tile, q, n, count),
            dst_ref=rows_of(tile, q, n, count),
            send_sem=c_send.at[at],
            recv_sem=c_recv.at[at],
            device_id=sibling,
            device_id_type=MESH,
        )

    def distance(i):
        return (1 - i % 2) * (1 + i // 2) + (i % 2) * (7 - i // 2)

    def send_own(n):
        @pl.loop(0, 7)
        def _(i):
            a_copy(n, distance(i)).start()

        c_copy(n, z, 0, 64).start()

    by_width(z + core, send_own)

    def add(i, total):
        at = columns(i)
        pltpu.make_async_copy(prior.at[:, at], prior.at[:, at], load_sem.at[i]).wait()
        s_high, s_low = parts(prior[:TILE, at])
        f_high, f_low = parts(prior[TILE:, at])
        return total + nt(
            jnp.concatenate([s_high, s_low], axis=0), jnp.concatenate([f_high, f_low], axis=0)
        )

    total = lax.fori_loop(0, chunks, add, jnp.zeros((128, 256), F32))
    sums = (total[:64, :128] + total[64:, 128:]) + (total[:64, 128:] + total[64:, :128])
    panel_parts[c] = pack(sums[:, :64])

    @pl.loop(1, 16)
    def _(k):
        over_col(panel_parts, 0, k).start()

    next_parts[c] = pack(sums[:, 64:])

    @pl.loop(1, 16)
    def _(k):
        over_col(under_parts, 1, k).start()

    def b_copy(n, at, d, q):
        tile = 2 * at + core
        if d < 2:
            to = ((x + (1 if d == 0 else 3)) % 4) * 4 + y
        else:
            to = x * 4 + (y + 1 + 2 * (at % 2)) % 4
        return pltpu.make_async_remote_copy(
            src_ref=rows_of(tile, q, n),
            dst_ref=rows_of(tile, q, n),
            send_sem=b_send.at[at],
            recv_sem=b_recv.at[at],
            device_id=(r, to),
            device_id_type=MESH,
        )

    def b_all(n, at):
        return pltpu.make_async_remote_copy(
            src_ref=whole.at[pl.ds(0, 48), pl.ds(0, 128 * n)],
            dst_ref=whole.at[pl.ds(0, 48), pl.ds(0, 128 * n)],
            send_sem=b_send.at[at],
            recv_sem=b_recv.at[at],
            device_id=(r, (c + 1) % 16),
            device_id_type=MESH,
        )

    def a_wait(n, at):
        tile = 2 * at + core
        pltpu.make_async_remote_copy(
            src_ref=rows_of(tile, quarter, n),
            dst_ref=rows_of(tile, quarter, n),
            send_sem=a_send.at[0],
            recv_sem=a_recv.at[at],
            device_id=(tile, c),
            device_id_type=MESH,
        ).wait_recv()

    def forward(i, carry):
        at = (z + distance(i)) % 8

        def one(n):
            a_wait(n, at)
            for d in range(3):
                b_copy(n, at, d, quarter).start()
            c_copy(n, at, quarter, 16).start()

        by_width(at + core, one)
        return carry

    lax.fori_loop(0, 4, forward, 0)

    all_col(panel_parts, 0).wait_recv()
    sum_1 = panel_parts[0]
    for k in range(1, 16):
        sum_1 = sum_1 + panel_parts[k]
    remaining = target[...] - unpack(sum_1)
    reduced[core, z] = pack(product(remaining, inverse[...], nt))

    def z_copy(k):
        return pltpu.make_async_remote_copy(
            src_ref=reduced.at[core, z],
            dst_ref=reduced.at[core, z],
            send_sem=z_sem.at[0],
            recv_sem=z_sem.at[1],
            device_id=(2 * ((z + k) % 8) + core, c),
            device_id_type=MESH,
        )

    all_z = pltpu.make_async_remote_copy(
        src_ref=reduced.at[core, pl.ds(0, 7)],
        dst_ref=reduced.at[core, pl.ds(0, 7)],
        send_sem=z_sem.at[0],
        recv_sem=z_sem.at[1],
        device_id=(2 * ((z + 1) % 8) + core, c),
        device_id_type=MESH,
    )
    pair = pltpu.make_async_remote_copy(
        src_ref=reduced.at[core],
        dst_ref=reduced.at[core],
        send_sem=pair_sem.at[0],
        recv_sem=pair_sem.at[1],
        device_id=sibling,
        device_id_type=MESH,
    )

    @pl.loop(1, 8)
    def _(k):
        z_copy(k).start()

    lax.fori_loop(4, 7, forward, 0)

    @pl.loop(1, 16)
    def _(k):
        over_col(next_parts, 2, k).start()

    def others(i, carry):
        at = (z + distance(i)) % 8

        def one(n):
            b_all(n, at).wait_recv()
            for step in range(1, 4):
                c_copy(n, at, (quarter + step) % 4, 16).start()

        by_width(at + core, one)
        return carry

    lax.fori_loop(0, 7, others, 0)

    all_z.wait_recv()
    pair.start()
    all_col(under_parts, 1).wait_recv()
    all_col(next_parts, 2).wait_recv()

    @pl.loop(0, 8)
    def _(at):
        def one(n):
            tile = 2 * at + 1 - core
            pltpu.make_async_remote_copy(
                src_ref=rows_of(tile, 0, n, 64),
                dst_ref=rows_of(tile, 0, n, 64),
                send_sem=c_send.at[at],
                recv_sem=c_recv.at[at],
                device_id=sibling,
                device_id_type=MESH,
            ).wait_recv()

        by_width(at + 1 - core, one)

    pair.wait_recv()

    for i, buffer in enumerate((panel_parts, under_parts, next_parts)):
        all_col(buffer, i).wait_send()
    all_z.wait_send()
    pair.wait_send()

    def own_sent(n):
        pltpu.make_async_remote_copy(
            src_ref=whole.at[pl.ds(0, 112), pl.ds(0, 128 * n)],
            dst_ref=whole.at[pl.ds(0, 112), pl.ds(0, 128 * n)],
            send_sem=a_send.at[0],
            recv_sem=a_recv.at[0],
            device_id=sibling,
            device_id_type=MESH,
        ).wait_send()

    by_width(z + core, own_sent)

    @pl.loop(0, 8)
    def _(at):
        def one(n):
            c_copy(n, at, 0, 64).wait_send()

            @pl.when(at != z)
            def _():
                b_all(n, at).wait_send()

        by_width(at + core, one)

    held = []
    for p in range(8):
        right = unpack_pair(reduced[0, p], reduced[1, p])
        link = whole[128 * p + 64 : 128 * p + 128, 128 * p : 128 * p + 128]
        link = link[:, :64]
        held.append(
            jnp.concatenate(
                [right[:, :64], right[:, 64:] - product(right[:, :64], link, nt)], axis=1
            )
        )
        if p > 0:
            even = whole[128 * p : 128 * p + 64, : 128 * p]
            odd = whole[128 * p + 64 : 128 * p + 128, : 128 * p]
            whole[128 * p + 64 : 128 * p + 128, : 128 * p] = odd - product(link, even, nn)

    later = jnp.zeros((64, 64), F32)
    for p in range(8):
        solved = held[p]
        reduced[0, p] = solved[:32]
        reduced[1, p] = solved[32:]
        if p < 7:
            change = product(
                solved, whole[128 * (p + 1) :, 128 * p : 128 * (p + 1)], nt
            )
            for m in range(p + 1, 8):
                at = 128 * (m - p - 1)
                held[m] = held[m] - change[:, at : at + 128]
        later = later + product(
            solved, unpack_pair(under_parts[2 * p], under_parts[2 * p + 1]), nt
        )

    mine = jnp.concatenate([reduced[0, z], reduced[1, z]], axis=0)
    own = jnp.where(core == 0, mine[:, :64], mine[:, 64:])
    sum_2 = next_parts[0]
    for k in range(1, 16):
        sum_2 = sum_2 + next_parts[k]
    remainder = next_target[...] - unpack(sum_2) - later
    out_ref[...] = jnp.concatenate([own, remainder], axis=1)


def local(*args):
    width = args[0].shape[1]
    chunks = width // CHUNK
    dma = pltpu.SemaphoreType.DMA
    out = pl.pallas_call(
        kernel,
        out_shape=jax.ShapeDtypeStruct((64, 128), F32),
        in_specs=[pl.BlockSpec(memory_space=pltpu.HBM)] * 8,
        out_specs=pl.BlockSpec(memory_space=pltpu.VMEM),
        scratch_shapes=[
            pltpu.VMEM((192, width), F32),
            pltpu.VMEM((64, 1024), F32),
            pltpu.VMEM((4, 64, 64), F32),
            pltpu.VMEM((1024, 1024), F32),
            pltpu.VMEM((16, 32, 128), F32),
            pltpu.VMEM((16, 32, 128), F32),
            pltpu.VMEM((16, 32, 128), F32),
            pltpu.VMEM((2, 8, 32, 128), F32),
            dma((chunks,)),
            dma((2,)),
            dma((3,)),
            dma((3,)),
            dma((2,)),
            dma((2,)),
            dma((1,)),
            dma((8,)),
            dma((8,)),
            dma((8,)),
            dma((8,)),
            dma((8,)),
        ],
        compiler_params=pltpu.CompilerParams(
            collective_id=0, has_side_effects=True, vmem_limit_bytes=60 * 1024 * 1024
        ),
    )(*args)
    return out[:, :64], out[:, 64:]


def solution(mesh):
    return jax.shard_map(
        local,
        mesh=mesh,
        in_specs=(
            P("row", "col"),
            P(None, "col"),
            P("row", None),
            P("row", None),
            P(None, "row"),
            P("row", "col"),
            P("row", "col"),
            P(None, "row"),
        ),
        out_specs=(P(None, "row"), P(None, "row")),
        check_vma=False,
    )
```

```python
import jax
import jax.numpy as jnp
from jax import lax
from jax.experimental import pallas as pl
from jax.experimental.pallas import tpu as pltpu
from jax.sharding import PartitionSpec as P

MESH = pl.DeviceIdType.MESH
TILE = 64
CHUNK = 2048
F32 = jnp.float32
BF16 = jnp.bfloat16


def nt(a, b):
    return lax.dot_general(a, b, (((1,), (1,)), ((), ())), preferred_element_type=F32)


def nn(a, b):
    return lax.dot_general(a, b, (((1,), (0,)), ((), ())), preferred_element_type=F32)


def parts(a):
    high = a.astype(BF16)
    return high, (a - high.astype(F32)).astype(BF16)


def product(a, b, dot):
    a_high, a_low = parts(a)
    b_high, b_low = parts(b)
    return dot(a_high, b_high) + (dot(a_high, b_low) + dot(a_low, b_high))


def pack(a):
    return jnp.concatenate([a[:32], a[32:]], axis=1)


def unpack(a):
    return jnp.concatenate([a[:, :64], a[:, 64:]], axis=0)


def unpack_pair(a, b):
    return jnp.concatenate(
        [
            jnp.concatenate([a[:, :64], b[:, :64]], axis=1),
            jnp.concatenate([a[:, 64:], b[:, 64:]], axis=1),
        ],
        axis=0,
    )


def kernel(
    factor_hbm,
    prior_hbm,
    lower_hbm,
    inverse_hbm,
    target_hbm,
    next_hbm,
    under_hbm,
    next_target_hbm,
    out_ref,
    prior,
    lower,
    small,
    whole,
    whole_high,
    whole_low,
    under_high,
    under_low,
    solved,
    panel_parts,
    next_parts,
    under_parts,
    reduced,
    load_sem,
    small_sem,
    col_send,
    col_recv,
    z_send,
    z_recv,
    pair_send,
    pair_recv,
    a_send,
    a_recv,
    b_send,
    b_recv,
    c_send,
    c_recv,
):
    r = lax.axis_index("row")
    c = lax.axis_index("col")
    z, core = r // 2, r % 2
    x, y = c // 4, c % 4
    quarter = (x + 2 * y) % 4
    sibling = (2 * z + 1 - core, c)
    chunks = prior.shape[1] // CHUNK

    pltpu.make_async_copy(lower_hbm, lower, small_sem.at[0]).start()
    for i, source in enumerate((inverse_hbm, under_hbm, target_hbm, next_target_hbm)):
        pltpu.make_async_copy(source, small.at[i], small_sem.at[1]).start()

    def columns(i):
        return pl.ds(pl.multiple_of(i * CHUNK, CHUNK), CHUNK)

    @pl.loop(0, chunks)
    def _(i):
        for j, source in enumerate((prior_hbm, factor_hbm, next_hbm)):
            pltpu.make_async_copy(
                source.at[:, columns(i)],
                prior.at[pl.ds(TILE * j, TILE), columns(i)],
                load_sem.at[i],
            ).start()

    barrier = pltpu.get_barrier_semaphore()

    @pl.loop(1, 16)
    def _(k):
        pl.semaphore_signal(barrier, inc=1, device_id=(r, (c + k) % 16), device_id_type=MESH)

    @pl.loop(1, 8)
    def _(k):
        pl.semaphore_signal(
            barrier, inc=1, device_id=(2 * ((z + k) % 8) + core, c), device_id_type=MESH
        )

    pl.semaphore_signal(barrier, inc=1, device_id=sibling, device_id_type=MESH)

    pltpu.make_async_copy(lower, lower, small_sem.at[0]).wait()
    pltpu.make_async_copy(small, small, small_sem.at[1]).wait()
    inverse, target, next_target = small.at[0], small.at[2], small.at[3]
    own_rows = pl.ds(pl.multiple_of(r * TILE, TILE), TILE)
    whole[own_rows, :] = product(inverse[...], lower[...], nn)
    under_parts[c] = pack(small[1])

    def add(i, total):
        at = columns(i)
        pltpu.make_async_copy(prior.at[:, at], prior.at[:, at], load_sem.at[i]).wait()
        s_high, s_low = parts(prior[:TILE, at])
        f_high, f_low = parts(prior[TILE:, at])
        return total + nt(
            jnp.concatenate([s_high, s_low], axis=0), jnp.concatenate([f_high, f_low], axis=0)
        )

    total = lax.fori_loop(0, 2, add, jnp.zeros((128, 256), F32))
    pl.semaphore_wait(barrier, 23)

    def over_col(buffer, i, k):
        return pltpu.make_async_remote_copy(
            src_ref=buffer.at[c],
            dst_ref=buffer.at[c],
            send_sem=col_send.at[i],
            recv_sem=col_recv.at[i],
            device_id=(r, (c + k) % 16),
            device_id_type=MESH,
        )

    def all_col(buffer, i):
        return pltpu.make_async_remote_copy(
            src_ref=buffer.at[pl.ds(0, 15)],
            dst_ref=buffer.at[pl.ds(0, 15)],
            send_sem=col_send.at[i],
            recv_sem=col_recv.at[i],
            device_id=(r, (c + 1) % 16),
            device_id_type=MESH,
        )

    def rows_of(tile, q, n, count=16):
        return whole.at[pl.ds(pl.multiple_of(tile * TILE + q * 16, 16), count), pl.ds(0, 128 * n)]

    def by_width(width, body):
        for n in range(1, 9):
            pl.when(width == n)(lambda n=n: body(n))

    def a_copy(n, k):
        return pltpu.make_async_remote_copy(
            src_ref=rows_of(r, quarter, n),
            dst_ref=rows_of(r, quarter, n),
            send_sem=a_send.at[0],
            recv_sem=a_recv.at[z],
            device_id=(2 * ((z + k) % 8) + core, c),
            device_id_type=MESH,
        )

    def c_copy(n, at, q, count):
        tile = 2 * at + core
        return pltpu.make_async_remote_copy(
            src_ref=rows_of(tile, q, n, count),
            dst_ref=rows_of(tile, q, n, count),
            send_sem=c_send.at[at],
            recv_sem=c_recv.at[at],
            device_id=sibling,
            device_id_type=MESH,
        )

    def send_own(n):
        @pl.loop(1, 8)
        def _(k):
            a_copy(n, k).start()

        c_copy(n, z, 0, 64).start()

    by_width(z + core, send_own)

    @pl.loop(1, 16)
    def _(k):
        over_col(under_parts, 1, k).start()

    total = lax.fori_loop(2, chunks, add, total)
    sums = (total[:64, :128] + total[64:, 128:]) + (total[:64, 128:] + total[64:, :128])
    panel_parts[c] = pack(sums[:, :64])

    @pl.loop(1, 16)
    def _(k):
        over_col(panel_parts, 0, k).start()

    next_parts[c] = pack(sums[:, 64:])

    def b_copy(n, at, d, q):
        tile = 2 * at + core
        if d < 2:
            to = ((x + (1 if d == 0 else 3)) % 4) * 4 + y
        else:
            to = x * 4 + (y + 1 + 2 * (at % 2)) % 4
        return pltpu.make_async_remote_copy(
            src_ref=rows_of(tile, q, n),
            dst_ref=rows_of(tile, q, n),
            send_sem=b_send.at[at],
            recv_sem=b_recv.at[at],
            device_id=(r, to),
            device_id_type=MESH,
        )

    def b_all(n, at):
        return pltpu.make_async_remote_copy(
            src_ref=whole.at[pl.ds(0, 48), pl.ds(0, 128 * n)],
            dst_ref=whole.at[pl.ds(0, 48), pl.ds(0, 128 * n)],
            send_sem=b_send.at[at],
            recv_sem=b_recv.at[at],
            device_id=(r, (c + 1) % 16),
            device_id_type=MESH,
        )

    def a_wait(n, at):
        tile = 2 * at + core
        pltpu.make_async_remote_copy(
            src_ref=rows_of(tile, quarter, n),
            dst_ref=rows_of(tile, quarter, n),
            send_sem=a_send.at[0],
            recv_sem=a_recv.at[at],
            device_id=(tile, c),
            device_id_type=MESH,
        ).wait_recv()

    def forward(half):
        @pl.loop(4 * half, 4 * half + 4)
        def _(at):
            def one(n):
                a_wait(n, at)
                for d in range(3):
                    b_copy(n, at, d, quarter).start()
                c_copy(n, at, quarter, 16).start()

            pl.when(at != z)(lambda: by_width(at + core, one))

    forward(0)
    pl.when(z >= 4)(lambda: forward(1))

    all_col(panel_parts, 0).wait_recv()
    sum_1 = panel_parts[0]
    for k in range(1, 16):
        sum_1 = sum_1 + panel_parts[k]
    remaining = target[...] - unpack(sum_1)
    reduced[core, z] = pack(product(remaining, inverse[...], nt))

    def z_copy(k):
        return pltpu.make_async_remote_copy(
            src_ref=reduced.at[core, z],
            dst_ref=reduced.at[core, z],
            send_sem=z_send.at[0],
            recv_sem=z_recv.at[z // 4],
            device_id=(2 * ((z + k) % 8) + core, c),
            device_id_type=MESH,
        )

    def z_all(count, half):
        return pltpu.make_async_remote_copy(
            src_ref=reduced.at[core, pl.ds(0, count)],
            dst_ref=reduced.at[core, pl.ds(0, count)],
            send_sem=z_send.at[0],
            recv_sem=z_recv.at[half],
            device_id=(2 * ((z + 1) % 8) + core, c),
            device_id_type=MESH,
        )

    def pair(half):
        return pltpu.make_async_remote_copy(
            src_ref=reduced.at[core, pl.ds(4 * half, 4)],
            dst_ref=reduced.at[core, pl.ds(4 * half, 4)],
            send_sem=pair_send.at[half],
            recv_sem=pair_recv.at[half],
            device_id=sibling,
            device_id_type=MESH,
        )

    @pl.loop(1, 8)
    def _(k):
        z_copy(k).start()

    pl.when(z < 4)(lambda: forward(1))

    @pl.loop(1, 16)
    def _(k):
        over_col(next_parts, 2, k).start()

    def others(half):
        @pl.loop(4 * half, 4 * half + 4)
        def _(at):
            def one(n):
                b_all(n, at).wait_recv()
                for step in range(1, 4):
                    c_copy(n, at, (quarter + step) % 4, 16).start()

            pl.when(at != z)(lambda: by_width(at + core, one))

    def to_sibling(half):
        pl.when(z // 4 == half)(lambda: z_all(3, half).wait_recv())
        pl.when(z // 4 != half)(lambda: z_all(4, half).wait_recv())
        pair(half).start()

    def from_sibling(half):
        @pl.loop(4 * half, 4 * half + 4)
        def _(at):
            def one(n):
                tile = 2 * at + 1 - core
                pltpu.make_async_remote_copy(
                    src_ref=rows_of(tile, 0, n, 64),
                    dst_ref=rows_of(tile, 0, n, 64),
                    send_sem=c_send.at[at],
                    recv_sem=c_recv.at[at],
                    device_id=sibling,
                    device_id_type=MESH,
                ).wait_recv()

            by_width(at + 1 - core, one)

    def prepare(half):
        links = []
        for p in range(4 * half, 4 * half + 4):
            even = slice(128 * p, 128 * p + 64)
            odd = slice(128 * p + 64, 128 * p + 128)
            link = parts(whole[odd, 128 * p : 128 * p + 128][:, :64])
            links.append(link)
            if p > 0:
                high, low = parts(whole[even, : 128 * p])
                whole_high[even, : 128 * p] = high
                whole_low[even, : 128 * p] = low
                change = nn(link[0], high) + (nn(link[0], low) + nn(link[1], high))
                high, low = parts(whole[odd, : 128 * p] - change)
                whole_high[odd, : 128 * p] = high
                whole_low[odd, : 128 * p] = low
        return links

    def times(a_high, a_low, b_high, b_low):
        m = a_high.shape[0]
        both = nt(jnp.concatenate([a_high, a_low], axis=0), b_high)
        return both[:m] + (both[m:] + nt(a_high, b_low))

    def start_of(half, links):
        held = []
        for p in range(4 * half, 4 * half + 4):
            right = unpack_pair(reduced[0, p], reduced[1, p])
            first = right[:, :64]
            change = times(*parts(first), *links[p - 4 * half])
            held.append(jnp.concatenate([first, right[:, 64:] - change], axis=1))
        return held

    def solve(half, held):
        highs, lows = [], []
        for i in range(4):
            p = 4 * half + i
            solved[p] = held[i]
            high, low = parts(held[i])
            highs.append(high)
            lows.append(low)
            if i < 3:
                rows = slice(128 * (p + 1), 512 * (half + 1))
                at = slice(128 * p, 128 * (p + 1))
                change = times(high, low, whole_high[rows, at], whole_low[rows, at])
                for m in range(i + 1, 4):
                    first = 128 * (m - i - 1)
                    held[m] = held[m] - change[:, first : first + 128]
        return jnp.concatenate(highs, axis=1), jnp.concatenate(lows, axis=1)

    others(0)
    to_sibling(0)
    from_sibling(0)
    links = prepare(0)
    pair(0).wait_recv()
    high, low = solve(0, start_of(0, links))

    others(1)
    all_col(under_parts, 1).wait_recv()
    for p in range(8):
        at = slice(128 * p, 128 * (p + 1))
        under_high[:, at], under_low[:, at] = parts(
            unpack_pair(under_parts[2 * p], under_parts[2 * p + 1])
        )
    later = times(high, low, under_high[:, :512], under_low[:, :512])
    from_sibling(1)
    links = prepare(1)
    known = times(high, low, whole_high[512:, :512], whole_low[512:, :512])

    all_col(next_parts, 2).wait_recv()
    sum_2 = next_parts[0]
    for k in range(1, 16):
        sum_2 = sum_2 + next_parts[k]
    later = next_target[...] - unpack(sum_2) - later

    for i, buffer in enumerate((panel_parts, under_parts, next_parts)):
        all_col(buffer, i).wait_send()
    z_all(7, 0).wait_send()
    pair(0).wait_send()

    def own_sent(n):
        pltpu.make_async_remote_copy(
            src_ref=whole.at[pl.ds(0, 112), pl.ds(0, 128 * n)],
            dst_ref=whole.at[pl.ds(0, 112), pl.ds(0, 128 * n)],
            send_sem=a_send.at[0],
            recv_sem=a_recv.at[0],
            device_id=sibling,
            device_id_type=MESH,
        ).wait_send()

    by_width(z + core, own_sent)

    @pl.loop(0, 8)
    def _(at):
        def one(n):
            c_copy(n, at, 0, 64).wait_send()
            pl.when(at != z)(lambda: b_all(n, at).wait_send())

        by_width(at + core, one)

    to_sibling(1)
    pair(1).wait_recv()
    held = [
        start - known[:, 128 * i : 128 * (i + 1)] for i, start in enumerate(start_of(1, links))
    ]
    high, low = solve(1, held)
    mine = solved[z]
    own = jnp.where(core == 0, mine[:, :64], mine[:, 64:])
    remainder = later - times(high, low, under_high[:, 512:], under_low[:, 512:])
    out_ref[...] = jnp.concatenate([own, remainder], axis=1)
    pair(1).wait_send()


def local(*args):
    width = args[0].shape[1]
    chunks = width // CHUNK
    dma = pltpu.SemaphoreType.DMA
    out = pl.pallas_call(
        kernel,
        out_shape=pltpu.VMEM((64, 128), F32),
        in_specs=[pl.BlockSpec(memory_space=pltpu.HBM)] * 8,
        out_specs=pl.BlockSpec(memory_space=pltpu.VMEM),
        scratch_shapes=[
            pltpu.VMEM((192, width), F32),
            pltpu.VMEM((64, 1024), F32),
            pltpu.VMEM((4, 64, 64), F32),
            pltpu.VMEM((1024, 1024), F32),
            pltpu.VMEM((1024, 1024), BF16),
            pltpu.VMEM((1024, 1024), BF16),
            pltpu.VMEM((64, 1024), BF16),
            pltpu.VMEM((64, 1024), BF16),
            pltpu.VMEM((8, 64, 128), F32),
            pltpu.VMEM((16, 32, 128), F32),
            pltpu.VMEM((16, 32, 128), F32),
            pltpu.VMEM((16, 32, 128), F32),
            pltpu.VMEM((2, 8, 32, 128), F32),
            dma((chunks,)),
            dma((2,)),
            dma((3,)),
            dma((3,)),
            dma((1,)),
            dma((2,)),
            dma((2,)),
            dma((2,)),
            dma((1,)),
            dma((8,)),
            dma((8,)),
            dma((8,)),
            dma((8,)),
            dma((8,)),
        ],
        compiler_params=pltpu.CompilerParams(
            collective_id=0, has_side_effects=True, vmem_limit_bytes=60 * 1024 * 1024
        ),
    )(*args)
    return out[:, :64], out[:, 64:]


def solution(mesh):
    return jax.shard_map(
        local,
        mesh=mesh,
        in_specs=(
            P("row", "col"),
            P(None, "col"),
            P("row", None),
            P("row", None),
            P(None, "row"),
            P("row", "col"),
            P("row", "col"),
            P(None, "row"),
        ),
        out_specs=(P(None, "row"), P(None, "row")),
        check_vma=False,
    )
```

```python
import jax
import jax.numpy as jnp
from jax import lax
from jax.experimental import pallas as pl
from jax.experimental.pallas import tpu as pltpu
from jax.sharding import PartitionSpec as P

MESH = pl.DeviceIdType.MESH
TILE = 64
CHUNK = 2048
F32 = jnp.float32
BF16 = jnp.bfloat16


def nt(a, b):
    return lax.dot_general(a, b, (((1,), (1,)), ((), ())), preferred_element_type=F32)


def nn(a, b):
    return lax.dot_general(a, b, (((1,), (0,)), ((), ())), preferred_element_type=F32)


def parts(a):
    high = a.astype(BF16)
    return high, (a - high.astype(F32)).astype(BF16)


def product(a, b, dot):
    a_high, a_low = parts(a)
    b_high, b_low = parts(b)
    return dot(a_high, b_high) + (dot(a_high, b_low) + dot(a_low, b_high))


def pack(a):
    return jnp.concatenate([a[:32], a[32:]], axis=1)


def unpack(a):
    return jnp.concatenate([a[:, :64], a[:, 64:]], axis=0)


def unpack_pair(a, b):
    return jnp.concatenate(
        [
            jnp.concatenate([a[:, :64], b[:, :64]], axis=1),
            jnp.concatenate([a[:, 64:], b[:, 64:]], axis=1),
        ],
        axis=0,
    )


def kernel(
    factor_hbm,
    prior_hbm,
    lower_hbm,
    inverse_hbm,
    target_hbm,
    next_hbm,
    under_hbm,
    next_target_hbm,
    out_ref,
    prior,
    lower,
    small,
    whole,
    whole_high,
    whole_low,
    under_high,
    under_low,
    solved,
    panel_parts,
    next_out,
    next_in,
    next_all,
    scaled,
    under_parts,
    reduced,
    load_sem,
    small_sem,
    col_send,
    col_recv,
    z_send,
    z_recv,
    pair_send,
    pair_recv,
    a_send,
    a_recv,
    b_send,
    b_recv,
    c_send,
    c_recv,
):
    r = lax.axis_index("row")
    c = lax.axis_index("col")
    z, core = r // 2, r % 2
    x, y = c // 4, c % 4
    quarter = (x + 2 * y) % 4
    sibling = (2 * z + 1 - core, c)
    chunks = prior.shape[1] // CHUNK

    pltpu.make_async_copy(lower_hbm, lower, small_sem.at[0]).start()
    for i, source in enumerate((inverse_hbm, under_hbm, target_hbm, next_target_hbm)):
        pltpu.make_async_copy(source, small.at[i], small_sem.at[1]).start()

    def columns(i):
        return pl.ds(pl.multiple_of(i * CHUNK, CHUNK), CHUNK)

    @pl.loop(0, chunks)
    def _(i):
        for j, source in enumerate((prior_hbm, factor_hbm, next_hbm)):
            pltpu.make_async_copy(
                source.at[:, columns(i)],
                prior.at[pl.ds(TILE * j, TILE), columns(i)],
                load_sem.at[i],
            ).start()

    barrier = pltpu.get_barrier_semaphore()

    @pl.loop(1, 16)
    def _(k):
        pl.semaphore_signal(barrier, inc=1, device_id=(r, (c + k) % 16), device_id_type=MESH)

    @pl.loop(1, 8)
    def _(k):
        pl.semaphore_signal(
            barrier, inc=1, device_id=(2 * ((z + k) % 8) + core, c), device_id_type=MESH
        )

    pl.semaphore_signal(barrier, inc=1, device_id=sibling, device_id_type=MESH)

    pltpu.make_async_copy(lower, lower, small_sem.at[0]).wait()
    pltpu.make_async_copy(small, small, small_sem.at[1]).wait()
    inverse, target, next_target = small.at[0], small.at[2], small.at[3]
    own_rows = pl.ds(pl.multiple_of(r * TILE, TILE), TILE)
    whole[own_rows, :] = product(inverse[...], lower[...], nn)
    under_parts[c] = pack(small[1])

    def add(i, total):
        at = columns(i)
        pltpu.make_async_copy(prior.at[:, at], prior.at[:, at], load_sem.at[i]).wait()
        s_high, s_low = parts(prior[:TILE, at])
        f_high, f_low = parts(prior[TILE:, at])
        return total + nt(
            jnp.concatenate([s_high, s_low], axis=0), jnp.concatenate([f_high, f_low], axis=0)
        )

    total = lax.fori_loop(0, chunks, add, jnp.zeros((128, 256), F32))
    pl.semaphore_wait(barrier, 23)

    def over_col(buffer, i, k):
        return pltpu.make_async_remote_copy(
            src_ref=buffer.at[c],
            dst_ref=buffer.at[c],
            send_sem=col_send.at[i],
            recv_sem=col_recv.at[i],
            device_id=(r, (c + k) % 16),
            device_id_type=MESH,
        )

    def all_col(buffer, i):
        return pltpu.make_async_remote_copy(
            src_ref=buffer.at[pl.ds(0, 15)],
            dst_ref=buffer.at[pl.ds(0, 15)],
            send_sem=col_send.at[i],
            recv_sem=col_recv.at[i],
            device_id=(r, (c + 1) % 16),
            device_id_type=MESH,
        )

    def rows_of(tile, q, n, count=16):
        return whole.at[pl.ds(pl.multiple_of(tile * TILE + q * 16, 16), count), pl.ds(0, 128 * n)]

    def by_width(width, body):
        for n in range(1, 9):
            pl.when(width == n)(lambda n=n: body(n))

    def a_copy(n, k):
        return pltpu.make_async_remote_copy(
            src_ref=rows_of(r, quarter, n),
            dst_ref=rows_of(r, quarter, n),
            send_sem=a_send.at[0],
            recv_sem=a_recv.at[z],
            device_id=(2 * ((z + k) % 8) + core, c),
            device_id_type=MESH,
        )

    def c_copy(n, at, q, count):
        tile = 2 * at + core
        return pltpu.make_async_remote_copy(
            src_ref=rows_of(tile, q, n, count),
            dst_ref=rows_of(tile, q, n, count),
            send_sem=c_send.at[at],
            recv_sem=c_recv.at[at],
            device_id=sibling,
            device_id_type=MESH,
        )

    def send_own(n):
        @pl.loop(1, 8)
        def _(k):
            a_copy(n, k).start()

        c_copy(n, z, 0, 64).start()

    sums = (total[:64, :128] + total[64:, 128:]) + (total[:64, 128:] + total[64:, :128])
    panel_parts[c] = pack(sums[:, :64])

    @pl.loop(1, 16)
    def _(k):
        over_col(panel_parts, 0, k).start()

    by_width(z + core, send_own)

    @pl.loop(1, 16)
    def _(k):
        over_col(under_parts, 1, k).start()

    packed = pack(sums[:, 64:])
    for k in range(16):
        next_out[k] = packed[2 * k : 2 * k + 2]
    next_in[c] = next_out[c]

    @pl.loop(1, 16)
    def _(k):
        to = (c + k) % 16
        pltpu.make_async_remote_copy(
            src_ref=next_out.at[to],
            dst_ref=next_in.at[c],
            send_sem=col_send.at[2],
            recv_sem=col_recv.at[2],
            device_id=(r, to),
            device_id_type=MESH,
        ).start()

    def b_copy(n, at, d, q):
        tile = 2 * at + core
        if d < 2:
            to = ((x + (1 if d == 0 else 3)) % 4) * 4 + y
        else:
            to = x * 4 + (y + 1 + 2 * (at % 2)) % 4
        return pltpu.make_async_remote_copy(
            src_ref=rows_of(tile, q, n),
            dst_ref=rows_of(tile, q, n),
            send_sem=b_send.at[at],
            recv_sem=b_recv.at[at],
            device_id=(r, to),
            device_id_type=MESH,
        )

    def b_all(n, at):
        return pltpu.make_async_remote_copy(
            src_ref=whole.at[pl.ds(0, 48), pl.ds(0, 128 * n)],
            dst_ref=whole.at[pl.ds(0, 48), pl.ds(0, 128 * n)],
            send_sem=b_send.at[at],
            recv_sem=b_recv.at[at],
            device_id=(r, (c + 1) % 16),
            device_id_type=MESH,
        )

    def a_wait(n, at):
        tile = 2 * at + core
        pltpu.make_async_remote_copy(
            src_ref=rows_of(tile, quarter, n),
            dst_ref=rows_of(tile, quarter, n),
            send_sem=a_send.at[0],
            recv_sem=a_recv.at[at],
            device_id=(tile, c),
            device_id_type=MESH,
        ).wait_recv()

    def forward(half):
        @pl.loop(4 * half, 4 * half + 4)
        def _(at):
            def one(n):
                a_wait(n, at)
                for d in range(3):
                    b_copy(n, at, d, quarter).start()
                c_copy(n, at, quarter, 16).start()

            pl.when(at != z)(lambda: by_width(at + core, one))

    forward(0)
    pl.when(z >= 4)(lambda: forward(1))

    all_col(panel_parts, 0).wait_recv()
    sum_1 = panel_parts[0]
    for k in range(1, 16):
        sum_1 = sum_1 + panel_parts[k]
    remaining = target[...] - unpack(sum_1)
    scaled[...] = product(remaining, inverse[...], nt)

    def z_copy(k):
        return pltpu.make_async_remote_copy(
            src_ref=reduced.at[core, z],
            dst_ref=reduced.at[core, z],
            send_sem=z_send.at[0],
            recv_sem=z_recv.at[z // 4],
            device_id=(2 * ((z + k) % 8) + core, c),
            device_id_type=MESH,
        )

    def z_all(count, half):
        return pltpu.make_async_remote_copy(
            src_ref=reduced.at[core, pl.ds(0, count)],
            dst_ref=reduced.at[core, pl.ds(0, count)],
            send_sem=z_send.at[0],
            recv_sem=z_recv.at[half],
            device_id=(2 * ((z + 1) % 8) + core, c),
            device_id_type=MESH,
        )

    def pair(half):
        return pltpu.make_async_remote_copy(
            src_ref=reduced.at[core, pl.ds(4 * half, 4)],
            dst_ref=reduced.at[core, pl.ds(4 * half, 4)],
            send_sem=pair_send.at[half],
            recv_sem=pair_recv.at[half],
            device_id=sibling,
            device_id_type=MESH,
        )

    def send_scaled(value):
        reduced[core, z] = pack(value)

        @pl.loop(1, 8)
        def _(k):
            z_copy(k).start()

    send_scaled(scaled[...])

    all_col(next_in, 2).wait_recv()
    sum_2 = next_in[0]
    for k in range(1, 16):
        sum_2 = sum_2 + next_in[k]
    next_all[c] = sum_2

    @pl.loop(1, 16)
    def _(k):
        over_col(next_all, 3, k).start()

    pl.when(z < 4)(lambda: forward(1))

    def others(half):
        @pl.loop(4 * half, 4 * half + 4)
        def _(at):
            def one(n):
                b_all(n, at).wait_recv()
                for step in range(1, 4):
                    c_copy(n, at, (quarter + step) % 4, 16).start()

            pl.when(at != z)(lambda: by_width(at + core, one))

    def to_sibling(half):
        pl.when(z // 4 == half)(lambda: z_all(3, half).wait_recv())
        pl.when(z // 4 != half)(lambda: z_all(4, half).wait_recv())
        pair(half).start()

    def from_sibling(half):
        @pl.loop(4 * half, 4 * half + 4)
        def _(at):
            def one(n):
                tile = 2 * at + 1 - core
                pltpu.make_async_remote_copy(
                    src_ref=rows_of(tile, 0, n, 64),
                    dst_ref=rows_of(tile, 0, n, 64),
                    send_sem=c_send.at[at],
                    recv_sem=c_recv.at[at],
                    device_id=sibling,
                    device_id_type=MESH,
                ).wait_recv()

            by_width(at + 1 - core, one)

    def prepare(half):
        links = []
        for p in range(4 * half, 4 * half + 4):
            even = slice(128 * p, 128 * p + 64)
            odd = slice(128 * p + 64, 128 * p + 128)
            link = parts(whole[odd, 128 * p : 128 * p + 128][:, :64])
            links.append(link)
            if p > 0:
                high, low = parts(whole[even, : 128 * p])
                whole_high[even, : 128 * p] = high
                whole_low[even, : 128 * p] = low
                change = nn(link[0], high) + (nn(link[0], low) + nn(link[1], high))
                high, low = parts(whole[odd, : 128 * p] - change)
                whole_high[odd, : 128 * p] = high
                whole_low[odd, : 128 * p] = low
        return links

    def times(a_high, a_low, b_high, b_low):
        m = a_high.shape[0]
        both = nt(jnp.concatenate([a_high, a_low], axis=0), b_high)
        return both[:m] + (both[m:] + nt(a_high, b_low))

    def start_of(half, links):
        held = []
        for p in range(4 * half, 4 * half + 4):
            right = unpack_pair(reduced[0, p], reduced[1, p])
            first = right[:, :64]
            change = times(*parts(first), *links[p - 4 * half])
            held.append(jnp.concatenate([first, right[:, 64:] - change], axis=1))
        return held

    def solve(half, held):
        highs, lows = [], []
        for i in range(4):
            p = 4 * half + i
            solved[p] = held[i]
            high, low = parts(held[i])
            highs.append(high)
            lows.append(low)
            if i < 3:
                rows = slice(128 * (p + 1), 512 * (half + 1))
                at = slice(128 * p, 128 * (p + 1))
                change = times(high, low, whole_high[rows, at], whole_low[rows, at])
                for m in range(i + 1, 4):
                    first = 128 * (m - i - 1)
                    held[m] = held[m] - change[:, first : first + 128]
        return jnp.concatenate(highs, axis=1), jnp.concatenate(lows, axis=1)

    others(0)
    to_sibling(0)
    from_sibling(0)
    links = prepare(0)
    pair(0).wait_recv()
    high, low = solve(0, start_of(0, links))

    others(1)
    all_col(under_parts, 1).wait_recv()
    for p in range(8):
        at = slice(128 * p, 128 * (p + 1))
        under_high[:, at], under_low[:, at] = parts(
            unpack_pair(under_parts[2 * p], under_parts[2 * p + 1])
        )
    later = times(high, low, under_high[:, :512], under_low[:, :512])
    from_sibling(1)
    links = prepare(1)
    known = times(high, low, whole_high[512:, :512], whole_low[512:, :512])

    all_col(next_all, 3).wait_recv()
    sum_2 = jnp.concatenate([next_all[k] for k in range(16)], axis=0)
    later = next_target[...] - unpack(sum_2) - later

    for i, buffer in enumerate((panel_parts, under_parts, next_out, next_all)):
        all_col(buffer, i).wait_send()
    z_all(7, 0).wait_send()
    pair(0).wait_send()

    def own_sent(n):
        pltpu.make_async_remote_copy(
            src_ref=whole.at[pl.ds(0, 112), pl.ds(0, 128 * n)],
            dst_ref=whole.at[pl.ds(0, 112), pl.ds(0, 128 * n)],
            send_sem=a_send.at[0],
            recv_sem=a_recv.at[0],
            device_id=sibling,
            device_id_type=MESH,
        ).wait_send()

    by_width(z + core, own_sent)

    @pl.loop(0, 8)
    def _(at):
        def one(n):
            c_copy(n, at, 0, 64).wait_send()
            pl.when(at != z)(lambda: b_all(n, at).wait_send())

        by_width(at + core, one)

    to_sibling(1)
    pair(1).wait_recv()
    held = [
        start - known[:, 128 * i : 128 * (i + 1)] for i, start in enumerate(start_of(1, links))
    ]
    high, low = solve(1, held)
    mine = solved[z]
    own = jnp.where(core == 0, mine[:, :64], mine[:, 64:])
    remainder = later - times(high, low, under_high[:, 512:], under_low[:, 512:])
    out_ref[...] = jnp.concatenate([own, remainder], axis=1)
    pair(1).wait_send()


def local(*args):
    width = args[0].shape[1]
    chunks = width // CHUNK
    dma = pltpu.SemaphoreType.DMA
    out = pl.pallas_call(
        kernel,
        out_shape=pltpu.VMEM((64, 128), F32),
        in_specs=[pl.BlockSpec(memory_space=pltpu.HBM)] * 8,
        out_specs=pl.BlockSpec(memory_space=pltpu.VMEM),
        scratch_shapes=[
            pltpu.VMEM((192, width), F32),
            pltpu.VMEM((64, 1024), F32),
            pltpu.VMEM((4, 64, 64), F32),
            pltpu.VMEM((1024, 1024), F32),
            pltpu.VMEM((1024, 1024), BF16),
            pltpu.VMEM((1024, 1024), BF16),
            pltpu.VMEM((64, 1024), BF16),
            pltpu.VMEM((64, 1024), BF16),
            pltpu.VMEM((8, 64, 128), F32),
            pltpu.VMEM((16, 32, 128), F32),
            pltpu.VMEM((16, 2, 128), F32),
            pltpu.VMEM((16, 2, 128), F32),
            pltpu.VMEM((16, 2, 128), F32),
            pltpu.VMEM((64, 64), F32),
            pltpu.VMEM((16, 32, 128), F32),
            pltpu.VMEM((2, 8, 32, 128), F32),
            dma((chunks,)),
            dma((2,)),
            dma((4,)),
            dma((4,)),
            dma((1,)),
            dma((2,)),
            dma((2,)),
            dma((2,)),
            dma((1,)),
            dma((8,)),
            dma((8,)),
            dma((8,)),
            dma((8,)),
            dma((8,)),
        ],
        compiler_params=pltpu.CompilerParams(
            collective_id=0, has_side_effects=True, vmem_limit_bytes=60 * 1024 * 1024
        ),
    )(*args)
    return out[:, :64], out[:, 64:]


def solution(mesh):
    return jax.shard_map(
        local,
        mesh=mesh,
        in_specs=(
            P("row", "col"),
            P(None, "col"),
            P("row", None),
            P("row", None),
            P(None, "row"),
            P("row", "col"),
            P("row", "col"),
            P(None, "row"),
        ),
        out_specs=(P(None, "row"), P(None, "row")),
        check_vma=False,
    )
```

```python
import jax
import jax.numpy as jnp
from jax import lax
from jax.experimental import pallas as pl
from jax.experimental.pallas import tpu as pltpu
from jax.sharding import PartitionSpec as P

MESH = pl.DeviceIdType.MESH
TILE = 64
CHUNK = 2048
F32 = jnp.float32
BF16 = jnp.bfloat16


def nt(a, b):
    return lax.dot_general(a, b, (((1,), (1,)), ((), ())), preferred_element_type=F32)


def nn(a, b):
    return lax.dot_general(a, b, (((1,), (0,)), ((), ())), preferred_element_type=F32)


def parts(a):
    high = a.astype(BF16)
    return high, (a - high.astype(F32)).astype(BF16)


def product(a, b, dot):
    a_high, a_low = parts(a)
    b_high, b_low = parts(b)
    return dot(a_high, b_high) + (dot(a_high, b_low) + dot(a_low, b_high))


def pack(a):
    return jnp.concatenate([a[:32], a[32:]], axis=1)


def unpack(a):
    return jnp.concatenate([a[:, :64], a[:, 64:]], axis=0)


def unpack_pair(a, b):
    return jnp.concatenate(
        [
            jnp.concatenate([a[:, :64], b[:, :64]], axis=1),
            jnp.concatenate([a[:, 64:], b[:, 64:]], axis=1),
        ],
        axis=0,
    )


def kernel(
    factor_hbm,
    prior_hbm,
    lower_hbm,
    inverse_hbm,
    target_hbm,
    next_hbm,
    under_hbm,
    next_target_hbm,
    out_ref,
    prior,
    lower,
    small,
    whole,
    whole_high,
    whole_low,
    under_high,
    under_low,
    solved,
    panel_parts,
    next_out,
    next_in,
    next_all,
    scaled,
    under_parts,
    reduced,
    load_sem,
    small_sem,
    col_send,
    col_recv,
    z_send,
    z_recv,
    pair_send,
    pair_recv,
    a_send,
    a_recv,
    b_send,
    b_recv,
    c_send,
    c_recv,
):
    r = lax.axis_index("row")
    c = lax.axis_index("col")
    z, core = r // 2, r % 2
    x, y = c // 4, c % 4
    quarter = (x + 2 * y) % 4
    sibling = (2 * z + 1 - core, c)
    chunks = prior.shape[1] // CHUNK

    pltpu.make_async_copy(lower_hbm, lower, small_sem.at[0]).start()
    for i, source in enumerate((inverse_hbm, under_hbm, target_hbm, next_target_hbm)):
        pltpu.make_async_copy(source, small.at[i], small_sem.at[1]).start()

    def columns(i):
        return pl.ds(pl.multiple_of(i * CHUNK, CHUNK), CHUNK)

    @pl.loop(0, chunks)
    def _(i):
        for j, source in enumerate((prior_hbm, factor_hbm, next_hbm)):
            pltpu.make_async_copy(
                source.at[:, columns(i)],
                prior.at[pl.ds(TILE * j, TILE), columns(i)],
                load_sem.at[i],
            ).start()

    barrier = pltpu.get_barrier_semaphore()

    @pl.loop(1, 16)
    def _(k):
        pl.semaphore_signal(barrier, inc=1, device_id=(r, (c + k) % 16), device_id_type=MESH)

    @pl.loop(1, 8)
    def _(k):
        pl.semaphore_signal(
            barrier, inc=1, device_id=(2 * ((z + k) % 8) + core, c), device_id_type=MESH
        )

    pl.semaphore_signal(barrier, inc=1, device_id=sibling, device_id_type=MESH)

    pltpu.make_async_copy(lower, lower, small_sem.at[0]).wait()
    pltpu.make_async_copy(small, small, small_sem.at[1]).wait()
    inverse, target, next_target = small.at[0], small.at[2], small.at[3]
    own_rows = pl.ds(pl.multiple_of(r * TILE, TILE), TILE)
    whole[own_rows, :] = product(inverse[...], lower[...], nn)
    under_parts[c] = pack(small[1])

    def add(i, total):
        at = columns(i)
        pltpu.make_async_copy(prior.at[:, at], prior.at[:, at], load_sem.at[i]).wait()
        s_high, s_low = parts(prior[:TILE, at])
        f_high, f_low = parts(prior[TILE:, at])
        return total + nt(
            jnp.concatenate([s_high, s_low], axis=0), jnp.concatenate([f_high, f_low], axis=0)
        )

    def over_col(buffer, i, k):
        return pltpu.make_async_remote_copy(
            src_ref=buffer.at[c],
            dst_ref=buffer.at[c],
            send_sem=col_send.at[i],
            recv_sem=col_recv.at[i],
            device_id=(r, (c + k) % 16),
            device_id_type=MESH,
        )

    def all_col(buffer, i):
        return pltpu.make_async_remote_copy(
            src_ref=buffer.at[pl.ds(0, 15)],
            dst_ref=buffer.at[pl.ds(0, 15)],
            send_sem=col_send.at[i],
            recv_sem=col_recv.at[i],
            device_id=(r, (c + 1) % 16),
            device_id_type=MESH,
        )

    def rows_of(tile, q, n, count=16):
        return whole.at[pl.ds(pl.multiple_of(tile * TILE + q * 16, 16), count), pl.ds(0, 128 * n)]

    def by_width(width, body):
        for n in range(1, 9):
            pl.when(width == n)(lambda n=n: body(n))

    def a_copy(n, k):
        return pltpu.make_async_remote_copy(
            src_ref=rows_of(r, quarter, n),
            dst_ref=rows_of(r, quarter, n),
            send_sem=a_send.at[0],
            recv_sem=a_recv.at[z],
            device_id=(2 * ((z + k) % 8) + core, c),
            device_id_type=MESH,
        )

    def c_copy(n, at, q, count):
        tile = 2 * at + core
        return pltpu.make_async_remote_copy(
            src_ref=rows_of(tile, q, n, count),
            dst_ref=rows_of(tile, q, n, count),
            send_sem=c_send.at[at],
            recv_sem=c_recv.at[at],
            device_id=sibling,
            device_id_type=MESH,
        )

    def send_own(n):
        @pl.loop(1, 8)
        def _(k):
            a_copy(n, k).start()

        c_copy(n, z, 0, 64).start()

    total = lax.fori_loop(0, 1, add, jnp.zeros((128, 256), F32))

    @pl.when(z >= 4)
    def _():
        pl.semaphore_wait(barrier, 23)
        by_width(z + core, send_own)

    total = lax.fori_loop(1, chunks, add, total)

    @pl.when(z < 4)
    def _():
        pl.semaphore_wait(barrier, 23)

    sums = (total[:64, :128] + total[64:, 128:]) + (total[:64, 128:] + total[64:, :128])
    panel_parts[c] = pack(sums[:, :64])

    @pl.loop(1, 16)
    def _(k):
        over_col(panel_parts, 0, k).start()

    pl.when(z < 4)(lambda: by_width(z + core, send_own))

    @pl.loop(1, 16)
    def _(k):
        over_col(under_parts, 1, k).start()

    packed = pack(sums[:, 64:])
    for k in range(16):
        next_out[k] = packed[2 * k : 2 * k + 2]
    next_in[c] = next_out[c]

    @pl.loop(1, 16)
    def _(k):
        to = (c + k) % 16
        pltpu.make_async_remote_copy(
            src_ref=next_out.at[to],
            dst_ref=next_in.at[c],
            send_sem=col_send.at[2],
            recv_sem=col_recv.at[2],
            device_id=(r, to),
            device_id_type=MESH,
        ).start()

    def b_copy(n, at, d, q):
        tile = 2 * at + core
        if d < 2:
            to = ((x + (1 if d == 0 else 3)) % 4) * 4 + y
        else:
            to = x * 4 + (y + 1 + 2 * (at % 2)) % 4
        return pltpu.make_async_remote_copy(
            src_ref=rows_of(tile, q, n),
            dst_ref=rows_of(tile, q, n),
            send_sem=b_send.at[at],
            recv_sem=b_recv.at[at],
            device_id=(r, to),
            device_id_type=MESH,
        )

    def b_all(n, at):
        return pltpu.make_async_remote_copy(
            src_ref=whole.at[pl.ds(0, 48), pl.ds(0, 128 * n)],
            dst_ref=whole.at[pl.ds(0, 48), pl.ds(0, 128 * n)],
            send_sem=b_send.at[at],
            recv_sem=b_recv.at[at],
            device_id=(r, (c + 1) % 16),
            device_id_type=MESH,
        )

    def a_wait(n, at):
        tile = 2 * at + core
        pltpu.make_async_remote_copy(
            src_ref=rows_of(tile, quarter, n),
            dst_ref=rows_of(tile, quarter, n),
            send_sem=a_send.at[0],
            recv_sem=a_recv.at[at],
            device_id=(tile, c),
            device_id_type=MESH,
        ).wait_recv()

    def forward(half):
        @pl.loop(4 * half, 4 * half + 4)
        def _(at):
            def one(n):
                a_wait(n, at)
                for d in range(3):
                    b_copy(n, at, d, quarter).start()
                c_copy(n, at, quarter, 16).start()

            pl.when(at != z)(lambda: by_width(at + core, one))

    forward(0)
    pl.when(z >= 4)(lambda: forward(1))

    all_col(panel_parts, 0).wait_recv()
    sum_1 = panel_parts[0]
    for k in range(1, 16):
        sum_1 = sum_1 + panel_parts[k]
    remaining = target[...] - unpack(sum_1)
    scaled[...] = product(remaining, inverse[...], nt)

    def z_copy(k):
        return pltpu.make_async_remote_copy(
            src_ref=reduced.at[core, z],
            dst_ref=reduced.at[core, z],
            send_sem=z_send.at[0],
            recv_sem=z_recv.at[z // 4],
            device_id=(2 * ((z + k) % 8) + core, c),
            device_id_type=MESH,
        )

    def z_all(count, half):
        return pltpu.make_async_remote_copy(
            src_ref=reduced.at[core, pl.ds(0, count)],
            dst_ref=reduced.at[core, pl.ds(0, count)],
            send_sem=z_send.at[0],
            recv_sem=z_recv.at[half],
            device_id=(2 * ((z + 1) % 8) + core, c),
            device_id_type=MESH,
        )

    def pair(half):
        return pltpu.make_async_remote_copy(
            src_ref=reduced.at[core, pl.ds(4 * half, 4)],
            dst_ref=reduced.at[core, pl.ds(4 * half, 4)],
            send_sem=pair_send.at[half],
            recv_sem=pair_recv.at[half],
            device_id=sibling,
            device_id_type=MESH,
        )

    def send_scaled(value):
        reduced[core, z] = pack(value)

        @pl.loop(1, 8)
        def _(k):
            z_copy(k).start()

    send_scaled(scaled[...])

    all_col(next_in, 2).wait_recv()
    sum_2 = next_in[0]
    for k in range(1, 16):
        sum_2 = sum_2 + next_in[k]
    next_all[c] = sum_2

    @pl.loop(1, 16)
    def _(k):
        over_col(next_all, 3, k).start()

    pl.when(z < 4)(lambda: forward(1))

    def others(half):
        @pl.loop(4 * half, 4 * half + 4)
        def _(at):
            def one(n):
                b_all(n, at).wait_recv()
                for step in range(1, 4):
                    c_copy(n, at, (quarter + step) % 4, 16).start()

            pl.when(at != z)(lambda: by_width(at + core, one))

    def to_sibling(half):
        pl.when(z // 4 == half)(lambda: z_all(3, half).wait_recv())
        pl.when(z // 4 != half)(lambda: z_all(4, half).wait_recv())
        pair(half).start()

    def from_sibling(half):
        @pl.loop(4 * half, 4 * half + 4)
        def _(at):
            def one(n):
                tile = 2 * at + 1 - core
                pltpu.make_async_remote_copy(
                    src_ref=rows_of(tile, 0, n, 64),
                    dst_ref=rows_of(tile, 0, n, 64),
                    send_sem=c_send.at[at],
                    recv_sem=c_recv.at[at],
                    device_id=sibling,
                    device_id_type=MESH,
                ).wait_recv()

            by_width(at + 1 - core, one)

    def prepare(half):
        links = []
        for p in range(4 * half, 4 * half + 4):
            even = slice(128 * p, 128 * p + 64)
            odd = slice(128 * p + 64, 128 * p + 128)
            link = parts(whole[odd, 128 * p : 128 * p + 128][:, :64])
            links.append(link)
            if p > 0:
                high, low = parts(whole[even, : 128 * p])
                whole_high[even, : 128 * p] = high
                whole_low[even, : 128 * p] = low
                change = nn(link[0], high) + (nn(link[0], low) + nn(link[1], high))
                high, low = parts(whole[odd, : 128 * p] - change)
                whole_high[odd, : 128 * p] = high
                whole_low[odd, : 128 * p] = low
        return links

    def times(a_high, a_low, b_high, b_low):
        m = a_high.shape[0]
        both = nt(jnp.concatenate([a_high, a_low], axis=0), b_high)
        return both[:m] + (both[m:] + nt(a_high, b_low))

    def start_of(half, links):
        held = []
        for p in range(4 * half, 4 * half + 4):
            right = unpack_pair(reduced[0, p], reduced[1, p])
            first = right[:, :64]
            change = times(*parts(first), *links[p - 4 * half])
            held.append(jnp.concatenate([first, right[:, 64:] - change], axis=1))
        return held

    def solve(half, held):
        highs, lows = [], []
        for i in range(4):
            p = 4 * half + i
            solved[p] = held[i]
            high, low = parts(held[i])
            highs.append(high)
            lows.append(low)
            if i < 3:
                rows = slice(128 * (p + 1), 512 * (half + 1))
                at = slice(128 * p, 128 * (p + 1))
                change = times(high, low, whole_high[rows, at], whole_low[rows, at])
                for m in range(i + 1, 4):
                    first = 128 * (m - i - 1)
                    held[m] = held[m] - change[:, first : first + 128]
        return jnp.concatenate(highs, axis=1), jnp.concatenate(lows, axis=1)

    others(0)
    to_sibling(0)
    from_sibling(0)
    links = prepare(0)
    pair(0).wait_recv()
    high, low = solve(0, start_of(0, links))

    others(1)
    all_col(under_parts, 1).wait_recv()
    for p in range(8):
        at = slice(128 * p, 128 * (p + 1))
        under_high[:, at], under_low[:, at] = parts(
            unpack_pair(under_parts[2 * p], under_parts[2 * p + 1])
        )
    later = times(high, low, under_high[:, :512], under_low[:, :512])
    from_sibling(1)
    links = prepare(1)
    known = times(high, low, whole_high[512:, :512], whole_low[512:, :512])

    all_col(next_all, 3).wait_recv()
    sum_2 = jnp.concatenate([next_all[k] for k in range(16)], axis=0)
    later = next_target[...] - unpack(sum_2) - later

    for i, buffer in enumerate((panel_parts, under_parts, next_out, next_all)):
        all_col(buffer, i).wait_send()
    z_all(7, 0).wait_send()
    pair(0).wait_send()

    def own_sent(n):
        pltpu.make_async_remote_copy(
            src_ref=whole.at[pl.ds(0, 112), pl.ds(0, 128 * n)],
            dst_ref=whole.at[pl.ds(0, 112), pl.ds(0, 128 * n)],
            send_sem=a_send.at[0],
            recv_sem=a_recv.at[0],
            device_id=sibling,
            device_id_type=MESH,
        ).wait_send()

    by_width(z + core, own_sent)

    @pl.loop(0, 8)
    def _(at):
        def one(n):
            c_copy(n, at, 0, 64).wait_send()
            pl.when(at != z)(lambda: b_all(n, at).wait_send())

        by_width(at + core, one)

    to_sibling(1)
    pair(1).wait_recv()
    held = [
        start - known[:, 128 * i : 128 * (i + 1)] for i, start in enumerate(start_of(1, links))
    ]
    high, low = solve(1, held)
    mine = solved[z]
    own = jnp.where(core == 0, mine[:, :64], mine[:, 64:])
    remainder = later - times(high, low, under_high[:, 512:], under_low[:, 512:])
    out_ref[...] = jnp.concatenate([own, remainder], axis=1)
    pair(1).wait_send()


def local(*args):
    width = args[0].shape[1]
    chunks = width // CHUNK
    dma = pltpu.SemaphoreType.DMA
    out = pl.pallas_call(
        kernel,
        out_shape=pltpu.VMEM((64, 128), F32),
        in_specs=[pl.BlockSpec(memory_space=pltpu.HBM)] * 8,
        out_specs=pl.BlockSpec(memory_space=pltpu.VMEM),
        scratch_shapes=[
            pltpu.VMEM((192, width), F32),
            pltpu.VMEM((64, 1024), F32),
            pltpu.VMEM((4, 64, 64), F32),
            pltpu.VMEM((1024, 1024), F32),
            pltpu.VMEM((1024, 1024), BF16),
            pltpu.VMEM((1024, 1024), BF16),
            pltpu.VMEM((64, 1024), BF16),
            pltpu.VMEM((64, 1024), BF16),
            pltpu.VMEM((8, 64, 128), F32),
            pltpu.VMEM((16, 32, 128), F32),
            pltpu.VMEM((16, 2, 128), F32),
            pltpu.VMEM((16, 2, 128), F32),
            pltpu.VMEM((16, 2, 128), F32),
            pltpu.VMEM((64, 64), F32),
            pltpu.VMEM((16, 32, 128), F32),
            pltpu.VMEM((2, 8, 32, 128), F32),
            dma((chunks,)),
            dma((2,)),
            dma((4,)),
            dma((4,)),
            dma((1,)),
            dma((2,)),
            dma((2,)),
            dma((2,)),
            dma((1,)),
            dma((8,)),
            dma((8,)),
            dma((8,)),
            dma((8,)),
            dma((8,)),
        ],
        compiler_params=pltpu.CompilerParams(
            collective_id=0, has_side_effects=True, vmem_limit_bytes=60 * 1024 * 1024
        ),
    )(*args)
    return out[:, :64], out[:, 64:]


def solution(mesh):
    return jax.shard_map(
        local,
        mesh=mesh,
        in_specs=(
            P("row", "col"),
            P(None, "col"),
            P("row", None),
            P("row", None),
            P(None, "row"),
            P("row", "col"),
            P("row", "col"),
            P(None, "row"),
        ),
        out_specs=(P(None, "row"), P(None, "row")),
        check_vma=False,
    )
```

```python
import jax
import jax.numpy as jnp
from jax import lax
from jax.experimental import pallas as pl
from jax.experimental.pallas import tpu as pltpu
from jax.sharding import PartitionSpec as P

MESH = pl.DeviceIdType.MESH
TILE = 64
CHUNK = 2048
F32 = jnp.float32
BF16 = jnp.bfloat16


def nt(a, b):
    return lax.dot_general(a, b, (((1,), (1,)), ((), ())), preferred_element_type=F32)


def nn(a, b):
    return lax.dot_general(a, b, (((1,), (0,)), ((), ())), preferred_element_type=F32)


def parts(a):
    high = a.astype(BF16)
    return high, (a - high.astype(F32)).astype(BF16)


def product(a, b, dot):
    a_high, a_low = parts(a)
    b_high, b_low = parts(b)
    return dot(a_high, b_high) + (dot(a_high, b_low) + dot(a_low, b_high))


def pack(a):
    return jnp.concatenate([a[:32], a[32:]], axis=1)


def unpack(a):
    return jnp.concatenate([a[:, :64], a[:, 64:]], axis=0)


def unpack_pair(a, b):
    return jnp.concatenate(
        [
            jnp.concatenate([a[:, :64], b[:, :64]], axis=1),
            jnp.concatenate([a[:, 64:], b[:, 64:]], axis=1),
        ],
        axis=0,
    )


def kernel(
    factor_hbm,
    prior_hbm,
    lower_hbm,
    inverse_hbm,
    target_hbm,
    next_hbm,
    under_hbm,
    next_target_hbm,
    out_ref,
    prior,
    lower,
    small,
    whole,
    whole_high,
    whole_low,
    under_high,
    under_low,
    solved,
    panel_parts,
    next_out,
    next_in,
    next_all,
    scaled,
    under_parts,
    reduced,
    load_sem,
    small_sem,
    col_send,
    col_recv,
    z_send,
    z_recv,
    pair_send,
    pair_recv,
    a_send,
    a_recv,
    b_send,
    b_recv,
    c_send,
    c_recv,
):
    r = lax.axis_index("row")
    c = lax.axis_index("col")
    z, core = r // 2, r % 2
    x, y = c // 4, c % 4
    quarter = (x + 2 * y) % 4
    sibling = (2 * z + 1 - core, c)
    chunks = prior.shape[1] // CHUNK

    pltpu.make_async_copy(lower_hbm, lower, small_sem.at[0]).start()
    for i, source in enumerate((inverse_hbm, under_hbm, target_hbm, next_target_hbm)):
        pltpu.make_async_copy(source, small.at[i], small_sem.at[1]).start()

    def columns(i):
        return pl.ds(pl.multiple_of(i * CHUNK, CHUNK), CHUNK)

    @pl.loop(0, chunks)
    def _(i):
        for j, source in enumerate((prior_hbm, factor_hbm, next_hbm)):
            pltpu.make_async_copy(
                source.at[:, columns(i)],
                prior.at[pl.ds(TILE * j, TILE), columns(i)],
                load_sem.at[i],
            ).start()

    barrier = pltpu.get_barrier_semaphore()

    @pl.loop(1, 16)
    def _(k):
        pl.semaphore_signal(barrier, inc=1, device_id=(r, (c + k) % 16), device_id_type=MESH)

    @pl.loop(1, 8)
    def _(k):
        pl.semaphore_signal(
            barrier, inc=1, device_id=(2 * ((z + k) % 8) + core, c), device_id_type=MESH
        )

    pl.semaphore_signal(barrier, inc=1, device_id=sibling, device_id_type=MESH)

    pltpu.make_async_copy(lower, lower, small_sem.at[0]).wait()
    pltpu.make_async_copy(small, small, small_sem.at[1]).wait()
    inverse, target, next_target = small.at[0], small.at[2], small.at[3]
    own_rows = pl.ds(pl.multiple_of(r * TILE, TILE), TILE)
    whole[own_rows, :] = product(inverse[...], lower[...], nn)
    under_parts[c] = pack(small[1])

    def add(i, total):
        at = columns(i)
        pltpu.make_async_copy(prior.at[:, at], prior.at[:, at], load_sem.at[i]).wait()
        s_high, s_low = parts(prior[:TILE, at])
        f_high, f_low = parts(prior[TILE:, at])
        return total + nt(
            jnp.concatenate([s_high, s_low], axis=0), jnp.concatenate([f_high, f_low], axis=0)
        )

    def over_col(buffer, i, k):
        return pltpu.make_async_remote_copy(
            src_ref=buffer.at[c],
            dst_ref=buffer.at[c],
            send_sem=col_send.at[i],
            recv_sem=col_recv.at[i],
            device_id=(r, (c + k) % 16),
            device_id_type=MESH,
        )

    def all_col(buffer, i):
        return pltpu.make_async_remote_copy(
            src_ref=buffer.at[pl.ds(0, 15)],
            dst_ref=buffer.at[pl.ds(0, 15)],
            send_sem=col_send.at[i],
            recv_sem=col_recv.at[i],
            device_id=(r, (c + 1) % 16),
            device_id_type=MESH,
        )

    def rows_of(tile, q, n, count=16):
        return whole.at[pl.ds(pl.multiple_of(tile * TILE + q * 16, 16), count), pl.ds(0, 128 * n)]

    def by_width(width, body):
        for n in range(1, 9):
            pl.when(width == n)(lambda n=n: body(n))

    def a_copy(n, k):
        return pltpu.make_async_remote_copy(
            src_ref=rows_of(r, quarter, n),
            dst_ref=rows_of(r, quarter, n),
            send_sem=a_send.at[0],
            recv_sem=a_recv.at[z],
            device_id=(2 * ((z + k) % 8) + core, c),
            device_id_type=MESH,
        )

    def c_copy(n, at, q, count):
        tile = 2 * at + core
        return pltpu.make_async_remote_copy(
            src_ref=rows_of(tile, q, n, count),
            dst_ref=rows_of(tile, q, n, count),
            send_sem=c_send.at[at],
            recv_sem=c_recv.at[at],
            device_id=sibling,
            device_id_type=MESH,
        )

    def send_own(n):
        @pl.loop(1, 8)
        def _(k):
            a_copy(n, k).start()

        c_copy(n, z, 0, 64).start()

    total = lax.fori_loop(0, 1, add, jnp.zeros((128, 256), F32))

    @pl.when(z >= 4)
    def _():
        pl.semaphore_wait(barrier, 23)
        by_width(z + core, send_own)

    total = lax.fori_loop(1, chunks, add, total)

    @pl.when(z < 4)
    def _():
        pl.semaphore_wait(barrier, 23)

    sums = (total[:64, :128] + total[64:, 128:]) + (total[:64, 128:] + total[64:, :128])
    panel_parts[c] = pack(sums[:, :64])

    @pl.loop(1, 16)
    def _(k):
        over_col(panel_parts, 0, k).start()

    pl.when(z < 4)(lambda: by_width(z + core, send_own))

    packed = pack(sums[:, 64:])
    for k in range(16):
        next_out[k] = packed[2 * k : 2 * k + 2]
    next_in[c] = next_out[c]

    @pl.loop(1, 16)
    def _(k):
        to = (c + k) % 16
        pltpu.make_async_remote_copy(
            src_ref=next_out.at[to],
            dst_ref=next_in.at[c],
            send_sem=col_send.at[2],
            recv_sem=col_recv.at[2],
            device_id=(r, to),
            device_id_type=MESH,
        ).start()

    @pl.loop(1, 16)
    def _(k):
        over_col(under_parts, 1, k).start()

    def b_copy(n, at, d, q):
        tile = 2 * at + core
        if d < 2:
            to = ((x + (1 if d == 0 else 3)) % 4) * 4 + y
        else:
            to = x * 4 + (y + 1 + 2 * (at % 2)) % 4
        return pltpu.make_async_remote_copy(
            src_ref=rows_of(tile, q, n),
            dst_ref=rows_of(tile, q, n),
            send_sem=b_send.at[at],
            recv_sem=b_recv.at[at],
            device_id=(r, to),
            device_id_type=MESH,
        )

    def b_all(n, at):
        return pltpu.make_async_remote_copy(
            src_ref=whole.at[pl.ds(0, 48), pl.ds(0, 128 * n)],
            dst_ref=whole.at[pl.ds(0, 48), pl.ds(0, 128 * n)],
            send_sem=b_send.at[at],
            recv_sem=b_recv.at[at],
            device_id=(r, (c + 1) % 16),
            device_id_type=MESH,
        )

    def a_wait(n, at):
        tile = 2 * at + core
        pltpu.make_async_remote_copy(
            src_ref=rows_of(tile, quarter, n),
            dst_ref=rows_of(tile, quarter, n),
            send_sem=a_send.at[0],
            recv_sem=a_recv.at[at],
            device_id=(tile, c),
            device_id_type=MESH,
        ).wait_recv()

    def forward(half):
        @pl.loop(4 * half, 4 * half + 4)
        def _(at):
            def one(n):
                a_wait(n, at)
                for d in range(3):
                    b_copy(n, at, d, quarter).start()
                c_copy(n, at, quarter, 16).start()

            pl.when(at != z)(lambda: by_width(at + core, one))

    forward(0)
    pl.when(z >= 4)(lambda: forward(1))

    all_col(panel_parts, 0).wait_recv()
    sum_1 = panel_parts[0]
    for k in range(1, 16):
        sum_1 = sum_1 + panel_parts[k]
    remaining = target[...] - unpack(sum_1)
    scaled[...] = product(remaining, inverse[...], nt)

    def z_copy(k):
        return pltpu.make_async_remote_copy(
            src_ref=reduced.at[core, z],
            dst_ref=reduced.at[core, z],
            send_sem=z_send.at[0],
            recv_sem=z_recv.at[z // 4],
            device_id=(2 * ((z + k) % 8) + core, c),
            device_id_type=MESH,
        )

    def z_all(count, half):
        return pltpu.make_async_remote_copy(
            src_ref=reduced.at[core, pl.ds(0, count)],
            dst_ref=reduced.at[core, pl.ds(0, count)],
            send_sem=z_send.at[0],
            recv_sem=z_recv.at[half],
            device_id=(2 * ((z + 1) % 8) + core, c),
            device_id_type=MESH,
        )

    def pair(half):
        return pltpu.make_async_remote_copy(
            src_ref=reduced.at[core, pl.ds(4 * half, 4)],
            dst_ref=reduced.at[core, pl.ds(4 * half, 4)],
            send_sem=pair_send.at[half],
            recv_sem=pair_recv.at[half],
            device_id=sibling,
            device_id_type=MESH,
        )

    def send_scaled(value):
        reduced[core, z] = pack(value)

        @pl.loop(1, 8)
        def _(k):
            z_copy(k).start()

    send_scaled(scaled[...])

    all_col(next_in, 2).wait_recv()
    sum_2 = next_in[0]
    for k in range(1, 16):
        sum_2 = sum_2 + next_in[k]
    next_all[c] = sum_2

    @pl.loop(1, 16)
    def _(k):
        over_col(next_all, 3, k).start()

    pl.when(z < 4)(lambda: forward(1))

    def others(half):
        @pl.loop(4 * half, 4 * half + 4)
        def _(at):
            def one(n):
                b_all(n, at).wait_recv()
                for step in range(1, 4):
                    c_copy(n, at, (quarter + step) % 4, 16).start()

            pl.when(at != z)(lambda: by_width(at + core, one))

    def to_sibling(half):
        pl.when(z // 4 == half)(lambda: z_all(3, half).wait_recv())
        pl.when(z // 4 != half)(lambda: z_all(4, half).wait_recv())
        pair(half).start()

    def from_sibling(half):
        @pl.loop(4 * half, 4 * half + 4)
        def _(at):
            def one(n):
                tile = 2 * at + 1 - core
                pltpu.make_async_remote_copy(
                    src_ref=rows_of(tile, 0, n, 64),
                    dst_ref=rows_of(tile, 0, n, 64),
                    send_sem=c_send.at[at],
                    recv_sem=c_recv.at[at],
                    device_id=sibling,
                    device_id_type=MESH,
                ).wait_recv()

            by_width(at + 1 - core, one)

    def prepare(half):
        links = []
        for p in range(4 * half, 4 * half + 4):
            even = slice(128 * p, 128 * p + 64)
            odd = slice(128 * p + 64, 128 * p + 128)
            link = parts(whole[odd, 128 * p : 128 * p + 128][:, :64])
            links.append(link)
            if p > 0:
                high, low = parts(whole[even, : 128 * p])
                whole_high[even, : 128 * p] = high
                whole_low[even, : 128 * p] = low
                change = nn(link[0], high) + (nn(link[0], low) + nn(link[1], high))
                high, low = parts(whole[odd, : 128 * p] - change)
                whole_high[odd, : 128 * p] = high
                whole_low[odd, : 128 * p] = low
        return links

    def times(a_high, a_low, b_high, b_low):
        m = a_high.shape[0]
        both = nt(jnp.concatenate([a_high, a_low], axis=0), b_high)
        return both[:m] + (both[m:] + nt(a_high, b_low))

    def start_of(half, links):
        held = []
        for p in range(4 * half, 4 * half + 4):
            right = unpack_pair(reduced[0, p], reduced[1, p])
            first = right[:, :64]
            change = times(*parts(first), *links[p - 4 * half])
            held.append(jnp.concatenate([first, right[:, 64:] - change], axis=1))
        return held

    def solve(half, held):
        highs, lows = [], []
        for i in range(4):
            p = 4 * half + i
            solved[p] = held[i]
            high, low = parts(held[i])
            highs.append(high)
            lows.append(low)
            if i < 3:
                rows = slice(128 * (p + 1), 512 * (half + 1))
                at = slice(128 * p, 128 * (p + 1))
                change = times(high, low, whole_high[rows, at], whole_low[rows, at])
                for m in range(i + 1, 4):
                    first = 128 * (m - i - 1)
                    held[m] = held[m] - change[:, first : first + 128]
        return jnp.concatenate(highs, axis=1), jnp.concatenate(lows, axis=1)

    others(0)
    to_sibling(0)
    from_sibling(0)
    links = prepare(0)
    pair(0).wait_recv()
    high, low = solve(0, start_of(0, links))

    others(1)
    all_col(under_parts, 1).wait_recv()
    for p in range(8):
        at = slice(128 * p, 128 * (p + 1))
        under_high[:, at], under_low[:, at] = parts(
            unpack_pair(under_parts[2 * p], under_parts[2 * p + 1])
        )
    later = times(high, low, under_high[:, :512], under_low[:, :512])
    from_sibling(1)
    links = prepare(1)
    known = times(high, low, whole_high[512:, :512], whole_low[512:, :512])

    all_col(next_all, 3).wait_recv()
    sum_2 = jnp.concatenate([next_all[k] for k in range(16)], axis=0)
    later = next_target[...] - unpack(sum_2) - later

    for i, buffer in enumerate((panel_parts, under_parts, next_out, next_all)):
        all_col(buffer, i).wait_send()
    z_all(7, 0).wait_send()
    pair(0).wait_send()

    def own_sent(n):
        pltpu.make_async_remote_copy(
            src_ref=whole.at[pl.ds(0, 112), pl.ds(0, 128 * n)],
            dst_ref=whole.at[pl.ds(0, 112), pl.ds(0, 128 * n)],
            send_sem=a_send.at[0],
            recv_sem=a_recv.at[0],
            device_id=sibling,
            device_id_type=MESH,
        ).wait_send()

    by_width(z + core, own_sent)

    @pl.loop(0, 8)
    def _(at):
        def one(n):
            c_copy(n, at, 0, 64).wait_send()
            pl.when(at != z)(lambda: b_all(n, at).wait_send())

        by_width(at + core, one)

    to_sibling(1)
    pair(1).wait_recv()
    held = [
        start - known[:, 128 * i : 128 * (i + 1)] for i, start in enumerate(start_of(1, links))
    ]
    high, low = solve(1, held)
    mine = solved[z]
    own = jnp.where(core == 0, mine[:, :64], mine[:, 64:])
    remainder = later - times(high, low, under_high[:, 512:], under_low[:, 512:])
    out_ref[...] = jnp.concatenate([own, remainder], axis=1)
    pair(1).wait_send()


def local(*args):
    width = args[0].shape[1]
    chunks = width // CHUNK
    dma = pltpu.SemaphoreType.DMA
    out = pl.pallas_call(
        kernel,
        out_shape=pltpu.VMEM((64, 128), F32),
        in_specs=[pl.BlockSpec(memory_space=pltpu.HBM)] * 8,
        out_specs=pl.BlockSpec(memory_space=pltpu.VMEM),
        scratch_shapes=[
            pltpu.VMEM((192, width), F32),
            pltpu.VMEM((64, 1024), F32),
            pltpu.VMEM((4, 64, 64), F32),
            pltpu.VMEM((1024, 1024), F32),
            pltpu.VMEM((1024, 1024), BF16),
            pltpu.VMEM((1024, 1024), BF16),
            pltpu.VMEM((64, 1024), BF16),
            pltpu.VMEM((64, 1024), BF16),
            pltpu.VMEM((8, 64, 128), F32),
            pltpu.VMEM((16, 32, 128), F32),
            pltpu.VMEM((16, 2, 128), F32),
            pltpu.VMEM((16, 2, 128), F32),
            pltpu.VMEM((16, 2, 128), F32),
            pltpu.VMEM((64, 64), F32),
            pltpu.VMEM((16, 32, 128), F32),
            pltpu.VMEM((2, 8, 32, 128), F32),
            dma((chunks,)),
            dma((2,)),
            dma((4,)),
            dma((4,)),
            dma((1,)),
            dma((2,)),
            dma((2,)),
            dma((2,)),
            dma((1,)),
            dma((8,)),
            dma((8,)),
            dma((8,)),
            dma((8,)),
            dma((8,)),
        ],
        compiler_params=pltpu.CompilerParams(
            collective_id=0, has_side_effects=True, vmem_limit_bytes=60 * 1024 * 1024
        ),
    )(*args)
    return out[:, :64], out[:, 64:]


def solution(mesh):
    return jax.shard_map(
        local,
        mesh=mesh,
        in_specs=(
            P("row", "col"),
            P(None, "col"),
            P("row", None),
            P("row", None),
            P(None, "row"),
            P("row", "col"),
            P("row", "col"),
            P(None, "row"),
        ),
        out_specs=(P(None, "row"), P(None, "row")),
        check_vma=False,
    )
```
